256 devices in a mesh: comp: 2 (over x_hi), seq: 128 (over x_lo, z, y, core).
Axes of the slice: x: 4 (x_hi: 2, x_lo: 2; x = x_hi * 2 + x_lo), y: 4, z: 8, core: 2. Of those that a mesh axis runs over, the one named last changes fastest.
Arguments:
- stale_states: bfloat16 [2, 6144, 2432], P('comp', 'seq'), may hold values from -1.5 to 1.5
- mod_table: float32 [2, 28, 3, 2432], P('comp'), may hold values from -4.8 to 4.8
- timesteps: int32 [8], replicated, may hold values from 0 to 27
- text_count: int32 [8], replicated, may hold values from 64 to 128, as said below
- text_kv: bfloat16 [2, 1024, 1216], P(None, 'seq'), may hold values from -6 to 6
- qkv_weight: bfloat16 [2, 2432, 3648], P('comp', 'seq'), may hold values from -0.125 to 0.125
- out_weight: bfloat16 [2, 1216, 2432], P('comp', None, 'seq'), may hold values from -0.15625 to 0.15625
- qk_gain: float32 [2, 2, 1216], P('comp'), may hold values from 0.49 to 8.6
Outputs:
- new_states: bfloat16 [2, 6144, 2432], P('comp', 'seq')
The draws below stay inside these ranges and needn't reach their ends.
Inputs may be any that keep to these rules, and one draw needn't show every extreme that they name: `text_count`: one sequence uses all 128 slots.
All inputs are finite; a program needn't handle non-finite values.
Results may differ from the reference program's by a relative error of at most 0.0085.
The reference program's roundings to bfloat16 on the way (of `modulated`, `weights` and `attended`) count: a program that leaves them out, or rounds other values in their place, can miss the bound.
Values may be sent and summed in bfloat16 or wider, within the bound.
No kernel may reach another device: no remote copies, remote signals or barrier semaphores. Data moves between devices by JAX's collectives and lax.ppermute only.
A program may use at most 128 MiB of HBM per device.

```python
import jax
import jax.numpy as jnp
from jax import lax

D = 2432
HEADS = 19
HD = 64
STEPS = 28
HA = 1216
IMG = 768
TXT = 128
SEQS = 8
COMPS = 2


def draw_text_count(key, part):
    key = jax.random.fold_in(key, 5)
    first_draw, second_draw = jax.random.split(key)
    counts = jax.random.randint(first_draw, (SEQS,), TXT // 2, TXT + 1)
    chosen = jax.random.randint(second_draw, (), 0, SEQS)
    return jnp.where(jnp.arange(SEQS) == chosen, TXT, counts).astype(jnp.int32)


def draw_qk_gain(key, part):
    key = jax.random.fold_in(key, 11)
    cell_draw = jax.random.fold_in(key, 1)
    gains = jnp.exp(jax.random.uniform(cell_draw, (COMPS, 2, HEADS, HD), jnp.float32, -0.7, 0.7))
    return gains.reshape(COMPS, 2, HEADS * HD).astype(jnp.float32)


def with_ends(values, stream_key, smallest, top_value):
    spot = [jax.random.randint(jax.random.fold_in(stream_key, axis), (), 0, length) for axis, length in enumerate(values.shape)]
    longest = values.shape.index(max(values.shape))
    beside = spot[:longest] + [(spot[longest] + 1) % values.shape[longest]] + spot[longest + 1:]
    return values.at[tuple(spot)].set(smallest).at[tuple(beside)].set(top_value)


def block_levels(rng, extent, pieces, low, largest):
    loudness = 1.0
    for dim, parts in pieces:
        steps = jax.random.uniform(jax.random.fold_in(jax.random.fold_in(rng, 6), dim), (parts,), jnp.float32, low / len(pieces), largest / len(pieces))
        loudness = loudness * jnp.repeat(jnp.exp(steps), extent[dim] // parts).reshape((-1,) + (1,) * (len(extent) - 1 - dim))
    return loudness


def gaussian(key, dims, deviation, reach, shards=(), kind=jnp.bfloat16):
    factor_of = block_levels(key, dims, shards, -0.22, 0.18) if shards else 1.0
    array = jax.random.normal(key, dims, jnp.float32) * deviation * factor_of
    return jnp.minimum(jnp.maximum(array, -reach), reach).astype(kind)


def setup_inputs(seed: int = 0) -> dict:
    streams_of = jax.random.split(jax.random.key(seed), 9)
    return {
        "stale_states": gaussian(streams_of[0], (COMPS, SEQS * IMG, D), 0.25, 1.5, ((0, 2), (1, 128))),
        "mod_table": gaussian(streams_of[1], (COMPS, STEPS, 3, D), 0.8, 4.8, ((0, 2),), jnp.float32),
        "timesteps": with_ends(jax.random.randint(streams_of[2], (SEQS,), 0, STEPS), jax.random.fold_in(streams_of[2], 1), 0, STEPS - 1).astype(jnp.int32),
        "text_count": draw_text_count(jax.random.fold_in(streams_of[8], 71), 0),
        "text_kv": gaussian(streams_of[4], (2, SEQS * TXT, HA), 1.0, 6.0, ((1, 128),)),
        "qkv_weight": gaussian(streams_of[5], (COMPS, D, 3 * HA), D ** -0.5, 0.125, ((0, 2), (1, 128))),
        "out_weight": gaussian(streams_of[6], (COMPS, HA, D), HA ** -0.5, 0.15625, ((0, 2), (2, 128))),
        "qk_gain": draw_qk_gain(jax.random.fold_in(streams_of[8], 71), 0),
    }


EPSILON = 1e-06
MASKED = -1e+30

def head_norm(values, gain_row):
    shaped = values.reshape(values.shape[0], HEADS, HD)
    shaped = shaped * lax.rsqrt(lax.optimization_barrier(jnp.mean(shaped * shaped, axis=-1, keepdims=True)) + EPSILON)
    return shaped.reshape(values.shape[0], HEADS * HD) * gain_row

def reference(stale_states, mod_table, timesteps, text_count, text_kv, qkv_weight, out_weight, qk_gain):
    block_rows = 256 if IMG % 256 == 0 else IMG
    scale_factor = HD ** (-0.5)
    width_all = HEADS * HD

    def one_pair(flat_index):
        comp_index = flat_index // SEQS
        seq_index = flat_index % SEQS
        source = (comp_index + COMPS - 1) % COMPS
        states = lax.dynamic_slice(stale_states, (source, seq_index * IMG, jnp.int32(0)), (1, IMG, D))[0].astype(jnp.float32)
        step_index = lax.dynamic_index_in_dim(timesteps, seq_index, 0, False)
        comp_table = lax.dynamic_index_in_dim(mod_table, comp_index, 0, False)
        modulation = lax.dynamic_index_in_dim(comp_table, step_index, 0, False)
        centred = states - lax.optimization_barrier(jnp.mean(states, axis=-1, keepdims=True))
        normed = centred * lax.rsqrt(lax.optimization_barrier(jnp.mean(centred * centred, axis=-1, keepdims=True)) + EPSILON)
        modulated = (normed * (1.0 + modulation[1]) + modulation[0]).astype(jnp.bfloat16)
        projected = jnp.dot(modulated, lax.dynamic_index_in_dim(qkv_weight, comp_index, 0, False), preferred_element_type=jnp.float32)
        gain_rows = lax.dynamic_index_in_dim(qk_gain, comp_index, 0, False)
        queries = lax.optimization_barrier(head_norm(projected[:, :width_all], gain_rows[0]).astype(jnp.bfloat16))
        key_rows = lax.optimization_barrier(head_norm(projected[:, width_all:2 * width_all], gain_rows[1]).astype(jnp.bfloat16))
        values = lax.optimization_barrier(projected[:, 2 * width_all:].astype(jnp.bfloat16))
        text_part = lax.dynamic_slice(text_kv, (jnp.int32(0), seq_index * TXT, jnp.int32(0)), (2, TXT, width_all))
        all_keys = jnp.concatenate([key_rows, text_part[0]], 0).astype(jnp.float32).reshape(IMG + TXT, HEADS, HD)
        all_values = jnp.concatenate([values, text_part[1]], 0).astype(jnp.float32).reshape(IMG + TXT, HEADS, HD)
        text_valid = lax.dynamic_index_in_dim(text_count, seq_index, 0, False)
        key_bias = jnp.where(jnp.arange(IMG + TXT, dtype=jnp.int32) < IMG + text_valid, 0.0, MASKED).astype(jnp.float32)

        def attend(query_block):
            query_rows = query_block.astype(jnp.float32).reshape(block_rows, HEADS, HD)
            scores = jnp.einsum('qhd,khd->hqk', query_rows, all_keys) * scale_factor + key_bias
            row_peak = lax.optimization_barrier(jnp.max(scores, axis=-1, keepdims=True))
            exp_scores = jnp.exp(scores - row_peak)
            totals = lax.optimization_barrier(jnp.sum(exp_scores, axis=-1))
            weights = lax.optimization_barrier(exp_scores.astype(jnp.bfloat16)).astype(jnp.float32)
            mixed_sum = jnp.einsum('hqk,khd->qhd', weights, all_values)
            return (mixed_sum / jnp.transpose(totals)[:, :, None]).reshape(block_rows, width_all).astype(jnp.bfloat16)
        attended = lax.map(attend, queries.reshape(IMG // block_rows, block_rows, width_all)).reshape(IMG, width_all)
        branch = jnp.dot(attended, lax.dynamic_index_in_dim(out_weight, comp_index, 0, False), preferred_element_type=jnp.float32)
        return (states + modulation[2] * branch).astype(jnp.bfloat16)
    results = lax.map(one_pair, jnp.arange(COMPS * SEQS, dtype=jnp.int32))
    return results.reshape(COMPS, SEQS * IMG, D)
```

```python
import jax
import jax.numpy as jnp
import numpy as np
from jax import lax
from jax.experimental import pallas as pl
from jax.experimental.pallas import tpu as pltpu
from jax.sharding import Mesh
from jax.sharding import PartitionSpec as P

AXES = ("comp", "x", "z1", "z0", "y", "core")
SIZES = (2, 2, 4, 2, 4, 2)
SEQ = AXES[1:]
Z = ("z1", "z0")
HEADS = 19
HD = 64
YH = 5
YW = YH * HD
HALF = 512
TEXT_ROWS = 8
CHUNK = 152
SLOT = 160
EPSILON = 1e-06
MASKED = -1e30
BF16 = jnp.bfloat16
F32 = jnp.float32


def permuted(array, axis, by):
    devices = lax.axis_size(axis)
    return lax.ppermute(array, axis, [(i, (i + by) % devices) for i in range(devices)])


def beside_kernel(place_ref, mine_ref, other_ref, *refs):
    out_ref, room = refs[-2:]
    x = place_ref[0]
    used = mine_ref.shape[0]
    room[...] = jnp.zeros_like(room)
    mine, other = mine_ref[...].astype(F32), other_ref[...].astype(F32)
    room[:used, :] = jnp.where(x == 0, mine, other)
    room[used : 2 * used, :] = jnp.where(x == 0, other, mine)
    out_ref[...] = room[...].astype(BF16)


def arrange_kernel(gathered_ref, *refs):
    out_ref, room = refs[-2:]
    used = out_ref.shape[0] // gathered_ref.shape[0]
    for place in range(gathered_ref.shape[0]):
        room[place * used : (place + 1) * used, :] = gathered_ref[place].astype(F32)[:used]
    out_ref[...] = room[...].astype(BF16)


def prepare_kernel(weight_ref, text_ref, out_ref, room):
    weight_rows = weight_ref.shape[0]
    head_width = HEADS * HD
    room[...] = jnp.zeros_like(room)
    for y in range(4):
        first = y * YW
        split = HALF - YW
        for core in range(2):
            slot = y * 2 + core
            base = (core + 1) * head_width
            size = min(YW, head_width - first)
            room[slot, :weight_rows, :size] = weight_ref[:, base + first : base + first + size].astype(F32)
            begin = first + core * split
            query_size = min(YW - split if core else split, head_width - begin)
            room[slot, :weight_rows, YW : YW + query_size] = weight_ref[
                :, begin : begin + query_size
            ].astype(F32)
            text = text_ref[core, :, first : first + size].astype(F32)
            room[slot, 19:24, :size] = text[:5]
            room[slot, 19:22, YW:] = text[5:8, :split]
            if size > split:
                room[slot, 22:23, YW : YW + size - split] = text[5:6, split:size]
                room[slot, 23:24, YW : YW + size - split] = text[6:7, split:size]
                room[slot, 22:23, YW + 128 :] = text[7:8, split : split + 64]
            if size == YW:
                room[slot, 23:24, YW + 128 :] = text[7:8, split + 64 :]
    out_ref[...] = room[...].astype(BF16)


def compact_kernel(received_ref, *refs):
    block_ref, text_ref, rows_room, text_room = refs[-4:]
    split = HALF - YW
    rows_room[...] = jnp.zeros_like(rows_room)
    for source in range(8):
        value = received_ref[source].astype(F32)
        rows_room[source * 19 : (source + 1) * 19, :] = value[:19]
        at = source * TEXT_ROWS
        text_room[at : at + 5, :] = value[19:24, :YW]
        text_room[at + 5 : at + 8, :split] = value[19:22, YW:]
        text_room[at + 5 : at + 6, split:] = value[22:23, YW : YW + 128]
        text_room[at + 6 : at + 7, split:] = value[23:24, YW : YW + 128]
        text_room[at + 7 : at + 8, split : split + 64] = value[22:23, YW + 128 :]
        text_room[at + 7 : at + 8, split + 64 :] = value[23:24, YW + 128 :]
    block_ref[...] = rows_room[...].astype(BF16)
    text_ref[...] = text_room[...].astype(BF16)


def modulate_kernel(modulation_ref, raw_ref, *refs):
    h_ref = refs[-1]
    wide = raw_ref[...].astype(F32)
    centred = wide - jnp.mean(wide, axis=-1, keepdims=True)
    normed = centred * lax.rsqrt(jnp.mean(centred * centred, axis=-1, keepdims=True) + EPSILON)
    modulated = normed * (1.0 + modulation_ref[1:2, :]) + modulation_ref[0:1, :]
    modulated = modulated.astype(BF16)
    h_ref[...] = jnp.zeros_like(h_ref)
    for slot in range(16):
        h_ref[:, slot * SLOT : slot * SLOT + CHUNK] = modulated[:, slot * CHUNK : (slot + 1) * CHUNK]


def project_kernel(place_ref, gain_ref, plain_ref, h_ref, text_ref, *refs):
    blocks, (pairs_ref, queries_ref, whole) = refs[:16], refs[16:]
    for index, block in enumerate(blocks):
        whole[place_ref[4 + index]] = block[...]
    rows = h_ref.shape[0]
    pairs_ref[rows:, :] = text_ref[...]
    low = lax.broadcasted_iota(jnp.int32, (rows, 128), 1) < HD
    for tile in range(0, HALF, 256):
        weights = whole[:, :, tile : tile + 256].reshape(16 * SLOT, 256)
        product = jnp.dot(h_ref[...], weights, preferred_element_type=F32)
        for part in range(2):
            begin = tile + part * 128
            columns = slice(begin, begin + 128)
            value = product[:, part * 128 : part * 128 + 128]
            square = value * value
            low_sum = jnp.sum(jnp.where(low, square, 0.0), axis=-1, keepdims=True)
            high_sum = jnp.sum(jnp.where(low, 0.0, square), axis=-1, keepdims=True)
            mean = jnp.where(low, low_sum, high_sum) * (1.0 / HD)
            scaled = value * lax.rsqrt(mean + EPSILON) * gain_ref[:, columns]
            result = jnp.where(plain_ref[:, columns] > 0.0, value, scaled).astype(BF16)
            if begin + 128 <= YW:
                pairs_ref[:rows, columns] = result
            elif begin < YW:
                pairs_ref[:rows, begin:YW] = result[:, : YW - begin]
                queries_ref[:, : begin + 128 - YW] = result[:, YW - begin :]
            else:
                queries_ref[:, begin - YW : begin + 128 - YW] = result


def attend_kernel(place_ref, own, beside, own_q, beside_q, far, far_beside, out_ref, keys, values):
    core, z0, text_valid = place_ref[1], place_ref[2], place_ref[3]
    shard = own.shape[0]
    rows = out_ref.shape[0]
    image = shard - 8 * TEXT_ROWS
    for part, (mine, other) in enumerate(((own, beside), (far, far_beside))):
        at = slice(part * shard, (part + 1) * shard)

        @pl.when(core == 0)
        def _():
            keys[at, :] = mine[...]
            values[at, :] = other[...]

        @pl.when(core == 1)
        def _():
            keys[at, :] = other[...]
            values[at, :] = mine[...]

    column = lax.broadcasted_iota(jnp.int32, (1, 2 * shard), 1)
    is_far = column >= shard
    column = jnp.where(is_far, column - shard, column)
    slot = column - image + 8 * TEXT_ROWS * jnp.where(is_far, 1 - z0, z0)
    bias = jnp.where((column < image) | (slot < text_valid), 0.0, MASKED).astype(F32)
    split = HALF - YW
    each = rows // 4
    places = [pl.ds(pl.multiple_of((2 * y + core) * each, 16), each) for y in range(4)]
    mine, other = (
        jnp.concatenate([ref[at, :] for at in places], 0) for ref in (own_q, beside_q)
    )
    first = jnp.where(core == 0, mine, other)
    second = jnp.where(core == 0, other, mine)
    for head in range(YH):
        columns = slice(head * HD, (head + 1) * HD)
        if head * HD < split:
            queries = first[:, columns]
        else:
            queries = second[:, head * HD - split : (head + 1) * HD - split]
        scores = lax.dot_general(
            queries * BF16(HD**-0.5),
            keys[:, columns],
            (((1,), (1,)), ((), ())),
            preferred_element_type=F32,
        )
        scores = scores + bias
        peak = jnp.max(scores, axis=-1, keepdims=True)
        weights = jnp.exp(scores - peak)
        totals = jnp.sum(weights, axis=-1, keepdims=True)
        mixed = jnp.dot(weights.astype(BF16), values[:, columns], preferred_element_type=F32)
        out_ref[:, columns] = (mixed / totals).astype(BF16)


def finish_kernel(place_ref, a0, a1, a2, a3, own_ref, beside_ref, *refs):
    o0, o1, o2, o3, heads, result, weights = refs
    y, core = place_ref[0], place_ref[1]
    own, beside = own_ref[...].astype(F32), beside_ref[...].astype(F32)
    each = own.shape[0] // 16
    for part, value in enumerate(
        (jnp.where(core == 0, own, beside), jnp.where(core == 0, beside, own))
    ):
        for z in range(8):
            for x in range(2):
                at = ((x * 8 + z) * 2 + part) * each
                begin = (z * 2 + x) * each
                weights[at : at + each, :] = value[begin : begin + each]
    weight = weights[...].astype(BF16)
    for by, attended in enumerate((a0, a1, a2, a3)):
        heads[lax.rem(y + 4 - by, 4)] = attended[...]
    total = None
    for q in range(4):
        size = min(YW, HEADS * HD - q * YW)
        part = lax.dot_general(
            heads[q][:, :size],
            weight[:, q * YW : q * YW + size],
            (((1,), (1,)), ((), ())),
            preferred_element_type=F32,
        )
        total = part if total is None else total + part
    rows = o0.shape[0]
    result[...] = total.astype(BF16).reshape(4, rows, total.shape[1])
    for by, out_ref in enumerate((o0, o1, o2, o3)):
        out_ref[...] = result[lax.rem(y + by, 4)]


def assemble_kernel(place_ref, gate_ref, raw_ref, n0, n1, n2, n3, out_ref, branch):
    y = place_ref[0]
    run = n0.shape[1] // 16
    for by, part in enumerate((n0, n1, n2, n3)):
        value = part[...].astype(F32)
        for q in range(4):

            @pl.when(lax.rem(y + 4 - by, 4) == q)
            def _():
                for m in range(16):
                    at = (m * 4 + q) * run
                    branch[:, at : at + run] = value[:, m * run : (m + 1) * run]

    out_ref[...] = (raw_ref[...].astype(F32) + gate_ref[...] * branch[...]).astype(BF16)


def in_vmem(kernel, out_shape, args, flops=0, scratch=(), scalars=0, after=()):
    size = sum(a.size * a.dtype.itemsize for a in args)
    vmem = pl.BlockSpec(memory_space=pltpu.VMEM)
    return pl.pallas_call(
        kernel,
        out_shape=out_shape,
        in_specs=[pl.BlockSpec(memory_space=pltpu.SMEM)] * scalars
        + [vmem] * (len(args) - scalars)
        + [vmem] * len(after),
        out_specs=jax.tree.map(lambda _: vmem, out_shape),
        scratch_shapes=list(scratch),
        compiler_params=pltpu.CompilerParams(vmem_limit_bytes=16 * 1024 * 1024),
        cost_estimate=pl.CostEstimate(flops=flops, bytes_accessed=size, transcendentals=0),
    )(*args, *after)


def per_device(
    stale_states, mod_table, timesteps, text_count, text_kv, qkv_weight, out_weight, qk_gain
):
    rows, width = stale_states.shape[1:]
    head_width = HEADS * HD
    weight_rows = qkv_weight.shape[1]
    quarter = width // 4
    split = HALF - YW
    x, y, core, z0 = (lax.axis_index(name) for name in ("x", "y", "core", "z0"))
    z = lax.axis_index(Z)
    sequence = lax.axis_index(("x", "z1"))

    halves = in_vmem(
        prepare_kernel,
        jax.ShapeDtypeStruct((8, 24, HALF), BF16),
        (qkv_weight[0], text_kv),
        scratch=[pltpu.VMEM((8, 24, HALF), F32)],
    )
    received = lax.all_to_all(halves, ("y", "core"), split_axis=0, concat_axis=0, tiled=True)
    shard = jnp.transpose(out_weight[0])
    shard_beside = permuted(shard, "x", 1)

    raw = permuted(stale_states[0], "comp", 1)
    step_index = lax.dynamic_index_in_dim(timesteps, sequence, 0, False)
    modulation = lax.dynamic_index_in_dim(mod_table[0], step_index, 0, False)
    text_valid = lax.dynamic_index_in_dim(text_count, sequence, 0, False)
    gate = modulation[2:3]
    h = in_vmem(
        modulate_kernel,
        jax.ShapeDtypeStruct((rows, 16 * SLOT), BF16),
        (modulation, raw),
        after=(received, shard_beside),
    )
    block, text = in_vmem(
        compact_kernel,
        (
            jax.ShapeDtypeStruct((SLOT, HALF), BF16),
            jax.ShapeDtypeStruct((8 * TEXT_ROWS, YW), BF16),
        ),
        (received,),
        scratch=[pltpu.VMEM((SLOT, HALF), F32), pltpu.VMEM((8 * TEXT_ROWS, YW), F32)],
        after=(h,),
    )
    h = lax.all_gather(h, ("y", "core"), axis=0, tiled=True)

    gains = jnp.pad(qk_gain[0], ((0, 0), (0, 4 * YW - head_width)))
    gains = lax.dynamic_slice_in_dim(gains, y * YW, YW, 1)
    first_gain = jnp.concatenate([gains[1], gains[0, :split]])
    second_gain = jnp.concatenate(
        [jnp.ones((YW,), F32), gains[0, split:], jnp.ones((2 * HALF - 3 * YW,), F32)]
    )
    gain = jnp.where(core == 0, first_gain, second_gain)[None]
    plain = jnp.where((core == 1) & (jnp.arange(HALF) < YW), 1.0, 0.0).astype(F32)[None]

    ahead = lambda part: permuted(part, Z, 1)
    behind = lambda part: permuted(part, Z, 7)
    other = permuted(block, "x", 1)
    own_aheads, own_behinds = [ahead(block)], [behind(block)]
    other_aheads, other_behinds = [ahead(other)], [behind(other)]
    for step in range(2, 5):
        own_aheads.append(ahead(own_aheads[-1]))
        other_behinds.append(behind(other_behinds[-1]))
        if step < 4:
            own_behinds.append(behind(own_behinds[-1]))
            other_aheads.append(ahead(other_aheads[-1]))
    blocks = [(block, x, z), (other, 1 - x, z)]
    for step in range(1, 5):
        blocks.append((own_aheads[step - 1], x, z + 8 - step))
        blocks.append((other_behinds[step - 1], 1 - x, z + step))
        if step < 4:
            blocks.append((own_behinds[step - 1], x, z + step))
            blocks.append((other_aheads[step - 1], 1 - x, z + 8 - step))
    slots = [x_place * 8 + z_place % 8 for _, x_place, z_place in blocks]
    blocks = [part for part, _, _ in blocks]

    place = jnp.stack([y, core, z0, text_valid] + slots).astype(jnp.int32)
    both = in_vmem(
        beside_kernel,
        jax.ShapeDtypeStruct((56, head_width), BF16),
        (x.astype(jnp.int32)[None], shard, shard_beside),
        scratch=[pltpu.VMEM((56, head_width), F32)],
        scalars=1,
        after=(own_aheads[1], own_behinds[1], other_aheads[0], other_behinds[0]),
    )
    out_half = lax.all_gather(both, Z, axis=0, tiled=False)

    shard_rows = 8 * (rows + TEXT_ROWS)
    pairs, queries = in_vmem(
        project_kernel,
        (
            jax.ShapeDtypeStruct((shard_rows, YW), BF16),
            jax.ShapeDtypeStruct((8 * rows, split), BF16),
        ),
        (place, gain, plain, h, text, *blocks),
        flops=2 * 8 * rows * 16 * SLOT * HALF,
        scratch=[pltpu.VMEM((16, SLOT, HALF), BF16)],
        scalars=1,
    )

    far = permuted(pairs, "z0", 1)
    attended = in_vmem(
        attend_kernel,
        jax.ShapeDtypeStruct((4 * rows, YW), BF16),
        (
            place,
            pairs,
            permuted(pairs, "core", 1),
            queries,
            permuted(queries, "core", 1),
            far,
            permuted(far, "core", 1),
        ),
        flops=4 * 4 * rows * 2 * shard_rows * YW,
        scratch=[pltpu.VMEM((2 * shard_rows, YW), BF16)] * 2,
        scalars=1,
    )

    gathered = tuple(permuted(attended, "y", by) for by in (1, 2, 3))
    out_half = in_vmem(
        arrange_kernel,
        jax.ShapeDtypeStruct((16 * weight_rows, head_width), BF16),
        (out_half,),
        scratch=[pltpu.VMEM((16 * weight_rows, head_width), F32)],
        after=(attended,),
    )
    parts = in_vmem(
        finish_kernel,
        (jax.ShapeDtypeStruct((rows, quarter), BF16),) * 4,
        (place, attended)
        + gathered
        + (out_half, permuted(out_half, "core", 1)),
        flops=2 * 4 * rows * head_width * quarter,
        scratch=[
            pltpu.VMEM((4, 4 * rows, YW), BF16),
            pltpu.VMEM((4, rows, quarter), BF16),
            pltpu.VMEM((32 * weight_rows, head_width), F32),
        ],
        scalars=1,
    )
    parts = [parts[0]] + [permuted(parts[by], "y", by) for by in (1, 2, 3)]
    new = in_vmem(
        assemble_kernel,
        jax.ShapeDtypeStruct((rows, width), BF16),
        (place, gate, raw, *parts),
        scratch=[pltpu.VMEM((rows, width), F32)],
        scalars=1,
    )
    return new[None]


def solution(mesh):
    fine = Mesh(np.asarray(mesh.devices).reshape(SIZES), AXES)
    in_specs = (
        P("comp", SEQ, None),
        P("comp", None, None, None),
        P(),
        P(),
        P(None, SEQ, None),
        P("comp", SEQ, None),
        P("comp", None, SEQ),
        P("comp", None, None),
    )
    return jax.shard_map(
        per_device, mesh=fine, in_specs=in_specs, out_specs=P("comp", SEQ, None), check_vma=False
    )
```

```python
import jax
import jax.numpy as jnp
import numpy as np
from jax import lax
from jax.experimental import pallas as pl
from jax.experimental.pallas import tpu as pltpu
from jax.sharding import Mesh
from jax.sharding import PartitionSpec as P

AXES = ("comp", "x", "z1", "z0", "y", "core")
SIZES = (2, 2, 4, 2, 4, 2)
SEQ = AXES[1:]
Z = ("z1", "z0")
HEADS = 19
HD = 64
YH = 5
YW = YH * HD
HALF = 512
TEXT_ROWS = 8
CHUNK = 152
SLOT = 160
EPSILON = 1e-06
MASKED = -1e30
BF16 = jnp.bfloat16
F32 = jnp.float32


def permuted(array, axis, by):
    devices = lax.axis_size(axis)
    return lax.ppermute(array, axis, [(i, (i + by) % devices) for i in range(devices)])


def beside_kernel(place_ref, mine_ref, other_ref, *refs):
    out_ref, room = refs[-2:]
    x = place_ref[0]
    used = mine_ref.shape[0]
    room[...] = jnp.zeros_like(room)
    mine, other = mine_ref[...].astype(F32), other_ref[...].astype(F32)
    room[:used, :] = jnp.where(x == 0, mine, other)
    room[used : 2 * used, :] = jnp.where(x == 0, other, mine)
    out_ref[...] = room[...].astype(BF16)


def prepare_kernel(weight_ref, text_ref, out_ref, room):
    weight_rows = weight_ref.shape[0]
    head_width = HEADS * HD
    room[...] = jnp.zeros_like(room)
    for y in range(4):
        first = y * YW
        split = HALF - YW
        for core in range(2):
            slot = y * 2 + core
            base = (core + 1) * head_width
            size = min(YW, head_width - first)
            room[slot, :weight_rows, :size] = weight_ref[:, base + first : base + first + size].astype(F32)
            begin = first + core * split
            query_size = min(YW - split if core else split, head_width - begin)
            room[slot, :weight_rows, YW : YW + query_size] = weight_ref[
                :, begin : begin + query_size
            ].astype(F32)
            text = text_ref[core, :, first : first + size].astype(F32)
            room[slot, 19:24, :size] = text[:5]
            room[slot, 19:22, YW:] = text[5:8, :split]
            if size > split:
                room[slot, 22:23, YW : YW + size - split] = text[5:6, split:size]
                room[slot, 23:24, YW : YW + size - split] = text[6:7, split:size]
                room[slot, 22:23, YW + 128 :] = text[7:8, split : split + 64]
            if size == YW:
                room[slot, 23:24, YW + 128 :] = text[7:8, split + 64 :]
    out_ref[...] = room[...].astype(BF16)


def compact_kernel(received_ref, *refs):
    block_ref, text_ref, rows_room, text_room = refs[-4:]
    split = HALF - YW
    rows_room[...] = jnp.zeros_like(rows_room)
    for source in range(8):
        value = received_ref[source].astype(F32)
        rows_room[source * 19 : (source + 1) * 19, :] = value[:19]
        at = source * TEXT_ROWS
        text_room[at : at + 5, :] = value[19:24, :YW]
        text_room[at + 5 : at + 8, :split] = value[19:22, YW:]
        text_room[at + 5 : at + 6, split:] = value[22:23, YW : YW + 128]
        text_room[at + 6 : at + 7, split:] = value[23:24, YW : YW + 128]
        text_room[at + 7 : at + 8, split : split + 64] = value[22:23, YW + 128 :]
        text_room[at + 7 : at + 8, split + 64 :] = value[23:24, YW + 128 :]
    block_ref[...] = rows_room[...].astype(BF16)
    text_ref[...] = text_room[...].astype(BF16)


def modulate_kernel(modulation_ref, raw_ref, *refs):
    h_ref = refs[-1]
    wide = raw_ref[...].astype(F32)
    centred = wide - jnp.mean(wide, axis=-1, keepdims=True)
    normed = centred * lax.rsqrt(jnp.mean(centred * centred, axis=-1, keepdims=True) + EPSILON)
    modulated = normed * (1.0 + modulation_ref[1:2, :]) + modulation_ref[0:1, :]
    modulated = modulated.astype(BF16)
    h_ref[...] = jnp.zeros_like(h_ref)
    for slot in range(16):
        h_ref[:, slot * SLOT : slot * SLOT + CHUNK] = modulated[:, slot * CHUNK : (slot + 1) * CHUNK]


def project_kernel(place_ref, gain_ref, plain_ref, h_ref, text_ref, *refs):
    blocks, (pairs_ref, queries_ref, whole) = refs[:16], refs[16:]
    for index, block in enumerate(blocks):
        whole[place_ref[4 + index]] = block[...]
    rows = h_ref.shape[0]
    shard = pairs_ref.shape[0] * 2 // YH
    half = shard // 2
    pairs_ref[rows:shard, :] = text_ref[:, :128]
    pairs_ref[shard + rows : 2 * shard, :] = text_ref[:, 128:256]
    pairs_ref[shard + half + rows :, HD:] = text_ref[:, 256:]
    low = lax.broadcasted_iota(jnp.int32, (rows, 128), 1) < HD
    for tile in range(0, HALF, 256):
        weights = whole[:, :, tile : tile + 256].reshape(16 * SLOT, 256)
        product = jnp.dot(h_ref[...], weights, preferred_element_type=F32)
        for part in range(2):
            begin = tile + part * 128
            columns = slice(begin, begin + 128)
            value = product[:, part * 128 : part * 128 + 128]
            square = value * value
            low_sum = jnp.sum(jnp.where(low, square, 0.0), axis=-1, keepdims=True)
            high_sum = jnp.sum(jnp.where(low, 0.0, square), axis=-1, keepdims=True)
            mean = jnp.where(low, low_sum, high_sum) * (1.0 / HD)
            scaled = value * lax.rsqrt(mean + EPSILON) * gain_ref[:, columns]
            result = jnp.where(plain_ref[:, columns] > 0.0, value, scaled).astype(BF16)
            if begin + 128 <= YW:
                pairs_ref[begin // 128 * shard : begin // 128 * shard + rows, :] = result
            elif begin < YW:
                pairs_ref[2 * shard :, :HD] = result[:half, :HD]
                pairs_ref[2 * shard : shard + half + rows, HD:] = result[half:, :HD]
                queries_ref[:, :HD] = result[:, HD:]
            else:
                queries_ref[:, begin - YW : begin + 128 - YW] = result


def unpack(packed, room, part):
    shard = packed.shape[0] * 2 // YH
    half = shard // 2
    begin = part * shard
    room[0, begin : begin + shard, :] = packed[:shard, :]
    room[1, begin : begin + shard, :] = packed[shard : 2 * shard, :]
    room[2, begin : begin + half, :HD] = packed[2 * shard :, :HD]
    room[2, begin + half : begin + shard, :HD] = packed[2 * shard :, HD:]


def attend_kernel(place_ref, own, beside, own_q, beside_q, far, far_beside, out_ref, keys, values):
    core, z0, text_valid = place_ref[1], place_ref[2], place_ref[3]
    shard = own.shape[0] * 2 // YH
    rows = out_ref.shape[0] * 2 // YH
    image = shard - 8 * TEXT_ROWS
    for part, (mine, other) in enumerate(((own, beside), (far, far_beside))):

        @pl.when(core == 0)
        def _():
            unpack(mine, keys, part)
            unpack(other, values, part)

        @pl.when(core == 1)
        def _():
            unpack(other, keys, part)
            unpack(mine, values, part)

    column = lax.broadcasted_iota(jnp.int32, (1, 2 * shard), 1)
    is_far = column >= shard
    column = jnp.where(is_far, column - shard, column)
    slot = column - image + 8 * TEXT_ROWS * jnp.where(is_far, 1 - z0, z0)
    bias = jnp.where((column < image) | (slot < text_valid), 0.0, MASKED).astype(F32)
    split = HALF - YW
    each = rows // 4
    half = rows // 2
    places = [pl.ds(pl.multiple_of((2 * y + core) * each, 16), each) for y in range(4)]
    mine, other = (
        jnp.concatenate([ref[at, :] for at in places], 0) for ref in (own_q, beside_q)
    )
    first = jnp.where(core == 0, mine, other)
    second = jnp.where(core == 0, other, mine)
    for head in range(YH):
        columns = slice(head * HD, (head + 1) * HD)
        lanes = head % 2 * HD
        if head * HD < split:
            queries = first[:, columns]
        else:
            queries = second[:, head * HD - split : (head + 1) * HD - split]
        scores = lax.dot_general(
            queries * BF16(HD**-0.5),
            keys[head // 2, :, lanes : lanes + HD],
            (((1,), (1,)), ((), ())),
            preferred_element_type=F32,
        )
        scores = scores + bias
        peak = jnp.max(scores, axis=-1, keepdims=True)
        weights = jnp.exp(scores - peak)
        totals = jnp.sum(weights, axis=-1, keepdims=True)
        mixed = jnp.dot(
            weights.astype(BF16),
            values[head // 2, :, lanes : lanes + HD],
            preferred_element_type=F32,
        )
        attended = (mixed / totals).astype(BF16)
        at = head // 2 * rows
        if head < YH - 1:
            out_ref[at : at + rows, lanes : lanes + HD] = attended
        else:
            out_ref[at : at + half, :HD] = attended[:half]
            out_ref[at : at + half, HD:] = attended[half:]


def finish_kernel(place_ref, a0, a1, a2, a3, gathered_ref, *refs):
    o0, o1, o2, o3, heads, result, weights = refs
    y = place_ref[0]
    each = weights.shape[0] // 32
    gap = gathered_ref.shape[0] // 16
    for place in range(16):
        value = gathered_ref[place * gap : (place + 1) * gap, :].astype(F32)
        z, core = divmod(place, 2)
        for x in range(2):
            at = ((x * 8 + z) * 2 + core) * each
            weights[at : at + each, :] = value[x * each : (x + 1) * each]
    weight = weights[...].astype(BF16)
    rows = a0.shape[0] * 2 // YH
    half = rows // 2
    for by, attended in enumerate((a0, a1, a2, a3)):
        place = lax.rem(y + 4 - by, 4)
        heads[place, :, :128] = attended[:rows, :]
        heads[place, :, 128:256] = attended[rows : 2 * rows, :]
        heads[place, :half, 256:YW] = attended[2 * rows :, :HD]
        heads[place, half:, 256:YW] = attended[2 * rows :, HD:]
    total = None
    for q in range(4):
        size = min(YW, HEADS * HD - q * YW)
        part = lax.dot_general(
            heads[q][:, :size],
            weight[:, q * YW : q * YW + size],
            (((1,), (1,)), ((), ())),
            preferred_element_type=F32,
        )
        total = part if total is None else total + part
    rows = o0.shape[0]
    result[...] = total.astype(BF16).reshape(4, rows, total.shape[1])
    for by, out_ref in enumerate((o0, o1, o2, o3)):
        out_ref[...] = result[lax.rem(y + by, 4)]


def assemble_kernel(place_ref, gate_ref, raw_ref, n0, n1, n2, n3, out_ref, branch):
    y = place_ref[0]
    run = n0.shape[1] // 16
    for by, part in enumerate((n0, n1, n2, n3)):
        value = part[...].astype(F32)
        for q in range(4):

            @pl.when(lax.rem(y + 4 - by, 4) == q)
            def _():
                for m in range(16):
                    at = (m * 4 + q) * run
                    branch[:, at : at + run] = value[:, m * run : (m + 1) * run]

    out_ref[...] = (raw_ref[...].astype(F32) + gate_ref[...] * branch[...]).astype(BF16)


def in_vmem(kernel, out_shape, args, flops=0, scratch=(), scalars=0, after=()):
    size = sum(a.size * a.dtype.itemsize for a in args)
    vmem = pl.BlockSpec(memory_space=pltpu.VMEM)
    return pl.pallas_call(
        kernel,
        out_shape=out_shape,
        in_specs=[pl.BlockSpec(memory_space=pltpu.SMEM)] * scalars
        + [vmem] * (len(args) - scalars)
        + [vmem] * len(after),
        out_specs=jax.tree.map(lambda _: vmem, out_shape),
        scratch_shapes=list(scratch),
        compiler_params=pltpu.CompilerParams(vmem_limit_bytes=10 * 1024 * 1024),
        cost_estimate=pl.CostEstimate(flops=flops, bytes_accessed=size, transcendentals=0),
    )(*args, *after)


def per_device(
    stale_states, mod_table, timesteps, text_count, text_kv, qkv_weight, out_weight, qk_gain
):
    rows, width = stale_states.shape[1:]
    head_width = HEADS * HD
    weight_rows = qkv_weight.shape[1]
    quarter = width // 4
    split = HALF - YW
    x, y, core, z0 = (lax.axis_index(name) for name in ("x", "y", "core", "z0"))
    z = lax.axis_index(Z)
    sequence = lax.axis_index(("x", "z1"))

    halves = in_vmem(
        prepare_kernel,
        jax.ShapeDtypeStruct((8, 24, HALF), BF16),
        (qkv_weight[0], text_kv),
        scratch=[pltpu.VMEM((8, 24, HALF), F32)],
    )
    received = lax.all_to_all(halves, ("y", "core"), split_axis=0, concat_axis=0, tiled=True)
    shard = jnp.transpose(out_weight[0])
    shard_beside = permuted(shard, "x", 1)

    raw = permuted(stale_states[0], "comp", 1)
    step_index = lax.dynamic_index_in_dim(timesteps, sequence, 0, False)
    modulation = lax.dynamic_index_in_dim(mod_table[0], step_index, 0, False)
    text_valid = lax.dynamic_index_in_dim(text_count, sequence, 0, False)
    gate = modulation[2:3]
    h = in_vmem(
        modulate_kernel,
        jax.ShapeDtypeStruct((rows, 16 * SLOT), BF16),
        (modulation, raw),
        after=(shard_beside,),
    )
    block, text = in_vmem(
        compact_kernel,
        (
            jax.ShapeDtypeStruct((SLOT, HALF), BF16),
            jax.ShapeDtypeStruct((8 * TEXT_ROWS, YW), BF16),
        ),
        (received,),
        flops=7 * 10**10,
        scratch=[pltpu.VMEM((SLOT, HALF), F32), pltpu.VMEM((8 * TEXT_ROWS, YW), F32)],
        after=(h,),
    )
    h = lax.all_gather(h, ("y", "core"), axis=0, tiled=True)

    gains = jnp.pad(qk_gain[0], ((0, 0), (0, 4 * YW - head_width)))
    gains = lax.dynamic_slice_in_dim(gains, y * YW, YW, 1)
    first_gain = jnp.concatenate([gains[1], gains[0, :split]])
    second_gain = jnp.concatenate(
        [jnp.ones((YW,), F32), gains[0, split:], jnp.ones((2 * HALF - 3 * YW,), F32)]
    )
    gain = jnp.where(core == 0, first_gain, second_gain)[None]
    plain = jnp.where((core == 1) & (jnp.arange(HALF) < YW), 1.0, 0.0).astype(F32)[None]

    ahead = lambda part: permuted(part, Z, 1)
    behind = lambda part: permuted(part, Z, 7)
    other = permuted(block, "x", 1)
    own_aheads, own_behinds = [ahead(block)], [behind(block)]
    other_aheads, other_behinds = [ahead(other)], [behind(other)]
    for step in range(2, 5):
        own_aheads.append(ahead(own_aheads[-1]))
        other_behinds.append(behind(other_behinds[-1]))
        if step < 4:
            own_behinds.append(behind(own_behinds[-1]))
            other_aheads.append(ahead(other_aheads[-1]))
    blocks = [(block, x, z), (other, 1 - x, z)]
    for step in range(1, 5):
        blocks.append((own_aheads[step - 1], x, z + 8 - step))
        blocks.append((other_behinds[step - 1], 1 - x, z + step))
        if step < 4:
            blocks.append((own_behinds[step - 1], x, z + step))
            blocks.append((other_aheads[step - 1], 1 - x, z + 8 - step))
    slots = [x_place * 8 + z_place % 8 for _, x_place, z_place in blocks]
    blocks = [part for part, _, _ in blocks]

    place = jnp.stack([y, core, z0, text_valid] + slots).astype(jnp.int32)
    both = in_vmem(
        beside_kernel,
        jax.ShapeDtypeStruct((40, head_width), BF16),
        (x.astype(jnp.int32)[None], shard, shard_beside),
        scratch=[pltpu.VMEM((40, head_width), F32)],
        scalars=1,
        after=(own_aheads[1], own_behinds[1], other_aheads[0], other_behinds[0]),
    )
    out_columns = lax.all_gather(both, ("z1", "z0", "core"), axis=0, tiled=True)

    shard_rows = 8 * (rows + TEXT_ROWS)
    pairs, queries = in_vmem(
        project_kernel,
        (
            jax.ShapeDtypeStruct((shard_rows // 2 * YH, 128), BF16),
            jax.ShapeDtypeStruct((8 * rows, split), BF16),
        ),
        (place, gain, plain, h, text, *blocks),
        flops=2 * 8 * rows * 16 * SLOT * HALF,
        scratch=[pltpu.VMEM((16, SLOT, HALF), BF16)],
        scalars=1,
    )

    far = permuted(pairs, "z0", 1)
    attended = in_vmem(
        attend_kernel,
        jax.ShapeDtypeStruct((2 * rows * YH, 128), BF16),
        (
            place,
            pairs,
            permuted(pairs, "core", 1),
            queries,
            permuted(queries, "core", 1),
            far,
            permuted(far, "core", 1),
        ),
        flops=4 * 4 * rows * 2 * shard_rows * YW,
        scratch=[pltpu.VMEM((3, 2 * shard_rows, 128), BF16)] * 2,
        scalars=1,
    )

    gathered = tuple(permuted(attended, "y", by) for by in (1, 2, 3))
    parts = in_vmem(
        finish_kernel,
        (jax.ShapeDtypeStruct((rows, quarter), BF16),) * 4,
        (place, attended)
        + gathered
        + (out_columns,),
        flops=2 * 4 * rows * head_width * quarter,
        scratch=[
            pltpu.VMEM((4, 4 * rows, YW), BF16),
            pltpu.VMEM((4, rows, quarter), BF16),
            pltpu.VMEM((32 * weight_rows, head_width), F32),
        ],
        scalars=1,
    )
    parts = [parts[0]] + [permuted(parts[by], "y", by) for by in (1, 2, 3)]
    new = in_vmem(
        assemble_kernel,
        jax.ShapeDtypeStruct((rows, width), BF16),
        (place, gate, raw, *parts),
        scratch=[pltpu.VMEM((rows, width), F32)],
        scalars=1,
    )
    return new[None]


def solution(mesh):
    fine = Mesh(np.asarray(mesh.devices).reshape(SIZES), AXES)
    in_specs = (
        P("comp", SEQ, None),
        P("comp", None, None, None),
        P(),
        P(),
        P(None, SEQ, None),
        P("comp", SEQ, None),
        P("comp", None, SEQ),
        P("comp", None, None),
    )
    return jax.shard_map(
        per_device, mesh=fine, in_specs=in_specs, out_specs=P("comp", SEQ, None), check_vma=False
    )
```

```python
import jax
import jax.numpy as jnp
import numpy as np
from jax import lax
from jax.experimental import pallas as pl
from jax.experimental.pallas import tpu as pltpu
from jax.sharding import Mesh
from jax.sharding import PartitionSpec as P

AXES = ("comp", "x", "z1", "z0", "y", "core")
SIZES = (2, 2, 4, 2, 4, 2)
SEQ = AXES[1:]
Z = ("z1", "z0")
HEADS = 19
HD = 64
YH = 5
YW = YH * HD
HALF = 512
TEXT_ROWS = 8
CHUNK = 152
SLOT = 160
EPSILON = 1e-06
MASKED = -1e30
BF16 = jnp.bfloat16
F32 = jnp.float32


def permuted(array, axis, by):
    devices = lax.axis_size(axis)
    return lax.ppermute(array, axis, [(i, (i + by) % devices) for i in range(devices)])


def hold_kernel(array_ref, after_ref, out_ref):
    out_ref[...] = array_ref[...]


def hold(array, after):
    return in_vmem(
        hold_kernel, jax.ShapeDtypeStruct(array.shape, array.dtype), (array,), after=(after,)
    )


def beside_kernel(mine_ref, other_ref, *refs):
    out_ref, room = refs[-2:]
    x = lax.axis_index("x")
    used = mine_ref.shape[0]
    room[...] = jnp.zeros_like(room)
    mine, other = mine_ref[...].astype(F32), other_ref[...].astype(F32)
    room[:used, :] = jnp.where(x == 0, mine, other)
    room[used : 2 * used, :] = jnp.where(x == 0, other, mine)
    out_ref[...] = room[...].astype(BF16)


def prepare_kernel(weight_ref, text_ref, out_ref, room):
    weight_rows = weight_ref.shape[0]
    head_width = HEADS * HD
    room[...] = jnp.zeros_like(room)
    for y in range(4):
        first = y * YW
        split = HALF - YW
        for core in range(2):
            slot = y * 2 + core
            base = (core + 1) * head_width
            size = min(YW, head_width - first)
            room[slot, :weight_rows, :size] = weight_ref[:, base + first : base + first + size].astype(F32)
            begin = first + core * split
            query_size = min(YW - split if core else split, head_width - begin)
            room[slot, :weight_rows, YW : YW + query_size] = weight_ref[
                :, begin : begin + query_size
            ].astype(F32)
            text = text_ref[core, :, first : first + size].astype(F32)
            room[slot, 19:24, :size] = text[:5]
            room[slot, 19:22, YW:] = text[5:8, :split]
            if size > split:
                room[slot, 22:23, YW : YW + size - split] = text[5:6, split:size]
                room[slot, 23:24, YW : YW + size - split] = text[6:7, split:size]
                room[slot, 22:23, YW + 128 :] = text[7:8, split : split + 64]
            if size == YW:
                room[slot, 23:24, YW + 128 :] = text[7:8, split + 64 :]
    out_ref[...] = room[...].astype(BF16)


def compact_kernel(received_ref, *refs):
    block_ref, text_ref, rows_room, text_room = refs[-4:]
    split = HALF - YW
    for source in range(8):
        value = received_ref[source].astype(F32)
        rows_room[source * 19 : (source + 1) * 19, :] = value[:19]
        at = source * TEXT_ROWS
        text_room[at : at + 5, :] = value[19:24, :YW]
        text_room[at + 5 : at + 8, :split] = value[19:22, YW:]
        text_room[at + 5 : at + 6, split:] = value[22:23, YW : YW + 128]
        text_room[at + 6 : at + 7, split:] = value[23:24, YW : YW + 128]
        text_room[at + 7 : at + 8, split : split + 64] = value[22:23, YW + 128 :]
        text_room[at + 7 : at + 8, split + 64 :] = value[23:24, YW + 128 :]
    block_ref[...] = rows_room[...].astype(BF16)
    text_ref[...] = text_room[...].astype(BF16)


def modulate_kernel(steps_ref, raw_ref, table_ref, *refs):
    h_ref, gate_ref, modulation, arrived = refs[-4:]
    step = steps_ref[lax.axis_index("x") * 4 + lax.axis_index("z1")]
    copy = pltpu.make_async_copy(table_ref.at[step], modulation, arrived)
    copy.start()
    wide = raw_ref[...].astype(F32)
    centred = wide - jnp.mean(wide, axis=-1, keepdims=True)
    normed = centred * lax.rsqrt(jnp.mean(centred * centred, axis=-1, keepdims=True) + EPSILON)
    copy.wait()
    gate_ref[...] = modulation[2]
    modulated = normed * (1.0 + modulation[1]) + modulation[0]
    modulated = modulated.astype(BF16)
    h_ref[...] = jnp.zeros_like(h_ref)
    for slot in range(16):
        h_ref[:, slot * SLOT : slot * SLOT + CHUNK] = modulated[:, slot * CHUNK : (slot + 1) * CHUNK]


def places_of_blocks():
    x = lax.axis_index("x")
    z = lax.axis_index("z1") * 2 + lax.axis_index("z0")
    slots = [x * 8 + z, (1 - x) * 8 + z]
    for step in range(1, 5):
        slots += [x * 8 + lax.rem(z + 8 - step, 8), (1 - x) * 8 + lax.rem(z + step, 8)]
        if step < 4:
            slots += [x * 8 + lax.rem(z + step, 8), (1 - x) * 8 + lax.rem(z + 8 - step, 8)]
    return slots


def project_kernel(gains_ref, h_ref, text_ref, *refs):
    blocks, (pairs_ref, queries_ref, whole, gain_ref) = refs[:16], refs[16:]
    y, core = lax.axis_index("y"), lax.axis_index("core")
    split = HALF - YW
    gain_ref[...] = jnp.ones_like(gain_ref)
    for at in range(4):
        first = at * YW
        size = min(YW, HEADS * HD - first)

        @pl.when((y == at) & (core == 0))
        def _():
            gain_ref[:, :size] = gains_ref[1:2, first : first + size]
            gain_ref[:, YW:] = gains_ref[0:1, first : first + split]

        @pl.when((y == at) & (core == 1))
        def _():
            gain_ref[:, YW : YW + size - split] = gains_ref[0:1, first + split : first + size]

    whole[:, CHUNK:, :] = jnp.zeros((16, SLOT - CHUNK, HALF), BF16)
    for slot, block in zip(places_of_blocks(), blocks):
        whole[slot, :CHUNK, :] = block[...]
    rows = h_ref.shape[0]
    shard = pairs_ref.shape[0] * 2 // YH
    half = shard // 2
    pairs_ref[rows:shard, :] = text_ref[:, :128]
    pairs_ref[shard + rows : 2 * shard, :] = text_ref[:, 128:256]
    pairs_ref[shard + half + rows :, HD:] = text_ref[:, 256:]
    low = lax.broadcasted_iota(jnp.int32, (rows, 128), 1) < HD
    for tile in range(0, HALF, 256):
        weights = whole[:, :, tile : tile + 256].reshape(16 * SLOT, 256)
        product = jnp.dot(h_ref[...], weights, preferred_element_type=F32)
        for part in range(2):
            begin = tile + part * 128
            columns = slice(begin, begin + 128)
            value = product[:, part * 128 : part * 128 + 128]
            square = value * value
            low_sum = jnp.sum(jnp.where(low, square, 0.0), axis=-1, keepdims=True)
            high_sum = jnp.sum(jnp.where(low, 0.0, square), axis=-1, keepdims=True)
            mean = jnp.where(low, low_sum, high_sum) * (1.0 / HD)
            scaled = value * lax.rsqrt(mean + EPSILON) * gain_ref[:, columns]
            column = lax.broadcasted_iota(jnp.int32, (1, 128), 1) + begin
            plain = (core == 1) & (column < YW)
            result = jnp.where(plain, value, scaled).astype(BF16)
            if begin + 128 <= YW:
                pairs_ref[begin // 128 * shard : begin // 128 * shard + rows, :] = result
            elif begin < YW:
                pairs_ref[2 * shard :, :HD] = result[:half, :HD]
                pairs_ref[2 * shard : shard + half + rows, HD:] = result[half:, :HD]
                queries_ref[:, :HD] = result[:, HD:]
            else:
                queries_ref[:, begin - YW : begin + 128 - YW] = result


def unpack(packed, room, part):
    shard = packed.shape[0] * 2 // YH
    half = shard // 2
    begin = part * shard
    room[0, begin : begin + shard, :] = packed[:shard, :]
    room[1, begin : begin + shard, :] = packed[shard : 2 * shard, :]
    room[2, begin : begin + half, :HD] = packed[2 * shard :, :HD]
    room[2, begin + half : begin + shard, :HD] = packed[2 * shard :, HD:]


def attend_kernel(counts_ref, own, beside, own_q, beside_q, far, far_beside, out_ref, keys, values):
    core, z0 = lax.axis_index("core"), lax.axis_index("z0")
    text_valid = counts_ref[lax.axis_index("x") * 4 + lax.axis_index("z1")]
    shard = own.shape[0] * 2 // YH
    rows = out_ref.shape[0] * 2 // YH
    image = shard - 8 * TEXT_ROWS
    for part, (mine, other) in enumerate(((own, beside), (far, far_beside))):

        @pl.when(core == 0)
        def _():
            unpack(mine, keys, part)
            unpack(other, values, part)

        @pl.when(core == 1)
        def _():
            unpack(other, keys, part)
            unpack(mine, values, part)

    column = lax.broadcasted_iota(jnp.int32, (1, 2 * shard), 1)
    is_far = column >= shard
    column = jnp.where(is_far, column - shard, column)
    slot = column - image + 8 * TEXT_ROWS * jnp.where(is_far, 1 - z0, z0)
    bias = jnp.where((column < image) | (slot < text_valid), 0.0, MASKED).astype(F32)
    split = HALF - YW
    each = rows // 4
    half = rows // 2
    places = [pl.ds(pl.multiple_of((2 * y + core) * each, 16), each) for y in range(4)]
    mine, other = (
        jnp.concatenate([ref[at, :] for at in places], 0) for ref in (own_q, beside_q)
    )
    first = jnp.where(core == 0, mine, other)
    second = jnp.where(core == 0, other, mine)
    for head in range(YH):
        columns = slice(head * HD, (head + 1) * HD)
        lanes = head % 2 * HD
        if head * HD < split:
            queries = first[:, columns]
        else:
            queries = second[:, head * HD - split : (head + 1) * HD - split]
        scores = lax.dot_general(
            queries * BF16(HD**-0.5),
            keys[head // 2, :, lanes : lanes + HD],
            (((1,), (1,)), ((), ())),
            preferred_element_type=F32,
        )
        scores = scores + bias
        peak = jnp.max(scores, axis=-1, keepdims=True)
        weights = jnp.exp(scores - peak)
        totals = jnp.sum(weights, axis=-1, keepdims=True)
        mixed = jnp.dot(
            weights.astype(BF16),
            values[head // 2, :, lanes : lanes + HD],
            preferred_element_type=F32,
        )
        attended = (mixed / totals).astype(BF16)
        at = head // 2 * rows
        if head < YH - 1:
            out_ref[at : at + rows, lanes : lanes + HD] = attended
        else:
            out_ref[at : at + half, :HD] = attended[:half]
            out_ref[at : at + half, HD:] = attended[half:]


def arrange_kernel(gathered_ref, out_ref, weights):
    each = weights.shape[0] // 32
    gap = gathered_ref.shape[0] // 16
    for place in range(16):
        value = gathered_ref[place * gap : (place + 1) * gap, :].astype(F32)
        core, z = divmod(place, 8)
        for x in range(2):
            at = ((x * 8 + z) * 2 + core) * each
            weights[at : at + each, :] = value[x * each : (x + 1) * each]
    out_ref[...] = weights[...].astype(BF16)


def finish_kernel(a0, a1, a2, a3, weight_ref, o0, o1, o2, o3, heads, result):
    y = lax.axis_index("y")
    rows = a0.shape[0] * 2 // YH
    half = rows // 2
    for by, attended in enumerate((a0, a1, a2, a3)):
        place = lax.rem(y + 4 - by, 4)
        heads[place, :, :128] = attended[:rows, :]
        heads[place, :, 128:256] = attended[rows : 2 * rows, :]
        heads[place, :half, 256:YW] = attended[2 * rows :, :HD]
        heads[place, half:, 256:YW] = attended[2 * rows :, HD:]
    total = None
    for q in range(4):
        size = min(YW, HEADS * HD - q * YW)
        part = lax.dot_general(
            heads[q][:, :size],
            weight_ref[:, q * YW : q * YW + size],
            (((1,), (1,)), ((), ())),
            preferred_element_type=F32,
        )
        total = part if total is None else total + part
    rows = o0.shape[0]
    result[...] = total.astype(BF16).reshape(4, rows, total.shape[1])
    for by, out_ref in enumerate((o0, o1, o2, o3)):
        out_ref[...] = result[lax.rem(y + by, 4)]


def assemble_kernel(gate_ref, raw_ref, n0, n1, n2, n3, out_ref, branch):
    y = lax.axis_index("y")
    run = n0.shape[1] // 16
    for by, part in enumerate((n0, n1, n2, n3)):
        value = part[...].astype(F32)
        for q in range(4):

            @pl.when(lax.rem(y + 4 - by, 4) == q)
            def _():
                for m in range(16):
                    at = (m * 4 + q) * run
                    branch[:, at : at + run] = value[:, m * run : (m + 1) * run]

    out_ref[...] = (raw_ref[...].astype(F32) + gate_ref[...] * branch[...]).astype(BF16)


def in_vmem(kernel, out_shape, args, flops=0, scratch=(), scalars=0, after=(), anywhere=(), limit=8):
    size = sum(a.size * a.dtype.itemsize for a in args)
    vmem = pl.BlockSpec(memory_space=pltpu.VMEM)
    return pl.pallas_call(
        kernel,
        out_shape=out_shape,
        in_specs=[pl.BlockSpec(memory_space=pltpu.SMEM)] * scalars
        + [vmem] * (len(args) - scalars)
        + [pl.BlockSpec(memory_space=pl.ANY)] * len(anywhere)
        + [vmem] * len(after),
        out_specs=jax.tree.map(lambda _: vmem, out_shape),
        scratch_shapes=list(scratch),
        compiler_params=pltpu.CompilerParams(vmem_limit_bytes=limit * 1024 * 1024),
        cost_estimate=pl.CostEstimate(flops=flops, bytes_accessed=size, transcendentals=0),
    )(*args, *anywhere, *after)


def per_device(
    stale_states, mod_table, timesteps, text_count, text_kv, qkv_weight, out_weight, qk_gain
):
    rows, width = stale_states.shape[1:]
    head_width = HEADS * HD
    weight_rows = qkv_weight.shape[1]
    quarter = width // 4
    split = HALF - YW

    halves = in_vmem(
        prepare_kernel,
        jax.ShapeDtypeStruct((8, 24, HALF), BF16),
        (qkv_weight[0], text_kv),
        scratch=[pltpu.VMEM((8, 24, HALF), F32)],
    )
    received = lax.all_to_all(halves, ("y", "core"), split_axis=0, concat_axis=0, tiled=True)
    shard = jnp.transpose(out_weight[0])

    raw = permuted(stale_states[0], "comp", 1)
    h, gate = in_vmem(
        modulate_kernel,
        (
            jax.ShapeDtypeStruct((rows, 16 * SLOT), BF16),
            jax.ShapeDtypeStruct((1, width), F32),
        ),
        (timesteps, raw),
        scratch=[pltpu.VMEM((3, 1, width), F32), pltpu.SemaphoreType.DMA],
        scalars=1,
        anywhere=(mod_table.reshape(mod_table.shape[1:3] + (1, width)),),
        limit=60,
    )
    block, text = in_vmem(
        compact_kernel,
        (
            jax.ShapeDtypeStruct((CHUNK, HALF), BF16),
            jax.ShapeDtypeStruct((8 * TEXT_ROWS, YW), BF16),
        ),
        (received,),
        flops=7 * 10**10,
        scratch=[pltpu.VMEM((CHUNK, HALF), F32), pltpu.VMEM((8 * TEXT_ROWS, YW), F32)],
        after=(h,),
    )
    h = lax.all_gather(h, ("y", "core"), axis=0, tiled=True)

    ahead = lambda part: permuted(part, Z, 1)
    behind = lambda part: permuted(part, Z, 7)
    other = permuted(block, "x", 1)
    own_aheads, own_behinds = [ahead(block)], [behind(block)]
    other_aheads, other_behinds = [ahead(other)], [behind(other)]
    for step in range(2, 5):
        own_aheads.append(ahead(own_aheads[-1]))
        other_behinds.append(behind(other_behinds[-1]))
        if step < 4:
            own_behinds.append(behind(own_behinds[-1]))
            other_aheads.append(ahead(other_aheads[-1]))
    blocks = [block, other]
    for step in range(1, 5):
        blocks += [own_aheads[step - 1], other_behinds[step - 1]]
        if step < 4:
            blocks += [own_behinds[step - 1], other_aheads[step - 1]]

    shard_beside = permuted(hold(shard, block), "x", 1)
    both = in_vmem(
        beside_kernel,
        jax.ShapeDtypeStruct((40, head_width), BF16),
        (shard, shard_beside),
        scratch=[pltpu.VMEM((40, head_width), F32)],
        after=(own_aheads[1], own_behinds[1], other_aheads[0], other_behinds[0]),
    )
    out_columns = lax.all_gather(both, ("core", "z1", "z0"), axis=0, tiled=True)

    shard_rows = 8 * (rows + TEXT_ROWS)
    pairs, queries = in_vmem(
        project_kernel,
        (
            jax.ShapeDtypeStruct((shard_rows // 2 * YH, 128), BF16),
            jax.ShapeDtypeStruct((8 * rows, split), BF16),
        ),
        (qk_gain[0], h, text, *blocks),
        flops=2 * 8 * rows * 16 * SLOT * HALF,
        scratch=[
            pltpu.VMEM((16, SLOT, HALF), BF16),
            pltpu.VMEM((1, HALF), F32),
        ],
    )

    far = permuted(pairs, "z0", 1)
    attended = in_vmem(
        attend_kernel,
        jax.ShapeDtypeStruct((2 * rows * YH, 128), BF16),
        (
            text_count,
            pairs,
            permuted(pairs, "core", 1),
            queries,
            permuted(queries, "core", 1),
            far,
            permuted(far, "core", 1),
        ),
        flops=4 * 4 * rows * 2 * shard_rows * YW,
        scratch=[pltpu.VMEM((3, 2 * shard_rows, 128), BF16)] * 2,
        scalars=1,
    )

    out_columns = in_vmem(
        arrange_kernel,
        jax.ShapeDtypeStruct((32 * weight_rows, head_width), BF16),
        (out_columns,),
        flops=10**10,
        scratch=[pltpu.VMEM((32 * weight_rows, head_width), F32)],
    )
    gathered = tuple(permuted(attended, "y", by) for by in (1, 2, 3))
    parts = in_vmem(
        finish_kernel,
        (jax.ShapeDtypeStruct((rows, quarter), BF16),) * 4,
        (attended,)
        + gathered
        + (out_columns,),
        flops=2 * 4 * rows * head_width * quarter,
        scratch=[
            pltpu.VMEM((4, 4 * rows, YW), BF16),
            pltpu.VMEM((4, rows, quarter), BF16),
        ],
    )
    parts = [parts[0]] + [permuted(parts[by], "y", by) for by in (1, 2, 3)]
    new = in_vmem(
        assemble_kernel,
        jax.ShapeDtypeStruct((rows, width), BF16),
        (gate, raw, *parts),
        scratch=[pltpu.VMEM((rows, width), F32)],
    )
    return new[None]


def solution(mesh):
    fine = Mesh(np.asarray(mesh.devices).reshape(SIZES), AXES)
    in_specs = (
        P("comp", SEQ, None),
        P("comp", None, None, None),
        P(),
        P(),
        P(None, SEQ, None),
        P("comp", SEQ, None),
        P("comp", None, SEQ),
        P("comp", None, None),
    )
    return jax.shard_map(
        per_device, mesh=fine, in_specs=in_specs, out_specs=P("comp", SEQ, None), check_vma=False
    )
```

```python
import jax
import jax.numpy as jnp
import numpy as np
from jax import lax
from jax.experimental import pallas as pl
from jax.experimental.pallas import tpu as pltpu
from jax.sharding import Mesh
from jax.sharding import PartitionSpec as P

AXES = ("comp", "x", "z1", "z0", "y", "core")
SIZES = (2, 2, 4, 2, 4, 2)
SEQ = AXES[1:]
Z = ("z1", "z0")
HEADS = 19
HD = 64
YH = 5
YW = YH * HD
HALF = 512
TEXT_ROWS = 8
CHUNK = 152
SLOT = 160
EPSILON = 1e-06
MASKED = -1e30
BF16 = jnp.bfloat16
F32 = jnp.float32


def permuted(array, axis, by):
    devices = lax.axis_size(axis)
    return lax.ppermute(array, axis, [(i, (i + by) % devices) for i in range(devices)])


def hold_kernel(array_ref, after_ref, out_ref):
    out_ref[...] = array_ref[...]


def hold(array, after):
    return in_vmem(
        hold_kernel, jax.ShapeDtypeStruct(array.shape, array.dtype), (array,), after=(after,)
    )


def beside_kernel(mine_ref, other_ref, *refs):
    out_ref, room = refs[-2:]
    x = lax.axis_index("x")
    used = mine_ref.shape[0]
    room[...] = jnp.zeros_like(room)
    mine, other = mine_ref[...].astype(F32), other_ref[...].astype(F32)
    room[:used, :] = jnp.where(x == 0, mine, other)
    room[used : 2 * used, :] = jnp.where(x == 0, other, mine)
    out_ref[...] = room[...].astype(BF16)


def prepare_kernel(steps_ref, weight_ref, text_ref, table_ref, out_ref, picked_ref, room, arrived):
    step = steps_ref[lax.axis_index("x") * 4 + lax.axis_index("z1")]
    copy = pltpu.make_async_copy(table_ref.at[step], picked_ref, arrived)
    copy.start()
    weight_rows = weight_ref.shape[0]
    head_width = HEADS * HD
    room[...] = jnp.zeros_like(room)
    for y in range(4):
        first = y * YW
        split = HALF - YW
        for core in range(2):
            slot = y * 2 + core
            base = (core + 1) * head_width
            size = min(YW, head_width - first)
            room[slot, :weight_rows, :size] = weight_ref[:, base + first : base + first + size].astype(F32)
            begin = first + core * split
            query_size = min(YW - split if core else split, head_width - begin)
            room[slot, :weight_rows, YW : YW + query_size] = weight_ref[
                :, begin : begin + query_size
            ].astype(F32)
            text = text_ref[core, :, first : first + size].astype(F32)
            room[slot, 19:24, :size] = text[:5]
            room[slot, 19:22, YW:] = text[5:8, :split]
            if size > split:
                room[slot, 22:23, YW : YW + size - split] = text[5:6, split:size]
                room[slot, 23:24, YW : YW + size - split] = text[6:7, split:size]
                room[slot, 22:23, YW + 128 :] = text[7:8, split : split + 64]
            if size == YW:
                room[slot, 23:24, YW + 128 :] = text[7:8, split + 64 :]
    out_ref[...] = room[...].astype(BF16)
    copy.wait()


def compact_kernel(received_ref, *refs):
    block_ref, text_ref, rows_room, text_room = refs[-4:]
    split = HALF - YW
    for source in range(8):
        value = received_ref[source].astype(F32)
        rows_room[source * 19 : (source + 1) * 19, :] = value[:19]
        at = source * TEXT_ROWS
        text_room[at : at + 5, :] = value[19:24, :YW]
        text_room[at + 5 : at + 8, :split] = value[19:22, YW:]
        text_room[at + 5 : at + 6, split:] = value[22:23, YW : YW + 128]
        text_room[at + 6 : at + 7, split:] = value[23:24, YW : YW + 128]
        text_room[at + 7 : at + 8, split : split + 64] = value[22:23, YW + 128 :]
        text_room[at + 7 : at + 8, split + 64 :] = value[23:24, YW + 128 :]
    block_ref[...] = rows_room[...].astype(BF16)
    text_ref[...] = text_room[...].astype(BF16)


def modulate_kernel(modulation, raw_ref, h_ref):
    wide = raw_ref[...].astype(F32)
    centred = wide - jnp.mean(wide, axis=-1, keepdims=True)
    normed = centred * lax.rsqrt(jnp.mean(centred * centred, axis=-1, keepdims=True) + EPSILON)
    modulated = normed * (1.0 + modulation[1]) + modulation[0]
    modulated = modulated.astype(BF16)
    h_ref[...] = jnp.zeros_like(h_ref)
    for slot in range(16):
        h_ref[:, slot * SLOT : slot * SLOT + CHUNK] = modulated[:, slot * CHUNK : (slot + 1) * CHUNK]


def places_of_blocks():
    x = lax.axis_index("x")
    z = lax.axis_index("z1") * 2 + lax.axis_index("z0")
    slots = [x * 8 + z, (1 - x) * 8 + z]
    for step in range(1, 5):
        slots += [x * 8 + lax.rem(z + 8 - step, 8), (1 - x) * 8 + lax.rem(z + step, 8)]
        if step < 4:
            slots += [x * 8 + lax.rem(z + step, 8), (1 - x) * 8 + lax.rem(z + 8 - step, 8)]
    return slots


def project_kernel(gains_ref, h_ref, text_ref, *refs):
    blocks, (pairs_ref, queries_ref, whole, gain_ref) = refs[:16], refs[16:]
    y, core = lax.axis_index("y"), lax.axis_index("core")
    split = HALF - YW
    gain_ref[...] = jnp.ones_like(gain_ref)
    for at in range(4):
        first = at * YW
        size = min(YW, HEADS * HD - first)

        @pl.when((y == at) & (core == 0))
        def _():
            gain_ref[:, :size] = gains_ref[1:2, first : first + size]
            gain_ref[:, YW:] = gains_ref[0:1, first : first + split]

        @pl.when((y == at) & (core == 1))
        def _():
            gain_ref[:, YW : YW + size - split] = gains_ref[0:1, first + split : first + size]

    whole[:, CHUNK:, :] = jnp.zeros((16, SLOT - CHUNK, HALF), BF16)
    for slot, block in zip(places_of_blocks(), blocks):
        whole[slot, :CHUNK, :] = block[...]
    rows = h_ref.shape[0]
    shard = pairs_ref.shape[0] * 2 // YH
    half = shard // 2
    pairs_ref[rows:shard, :] = text_ref[:, :128]
    pairs_ref[shard + rows : 2 * shard, :] = text_ref[:, 128:256]
    pairs_ref[shard + half + rows :, HD:] = text_ref[:, 256:]
    low = lax.broadcasted_iota(jnp.int32, (rows, 128), 1) < HD
    for tile in range(0, HALF, 256):
        weights = whole[:, :, tile : tile + 256].reshape(16 * SLOT, 256)
        product = jnp.dot(h_ref[...], weights, preferred_element_type=F32)
        for part in range(2):
            begin = tile + part * 128
            columns = slice(begin, begin + 128)
            value = product[:, part * 128 : part * 128 + 128]
            square = value * value
            low_sum = jnp.sum(jnp.where(low, square, 0.0), axis=-1, keepdims=True)
            high_sum = jnp.sum(jnp.where(low, 0.0, square), axis=-1, keepdims=True)
            mean = jnp.where(low, low_sum, high_sum) * (1.0 / HD)
            scaled = value * lax.rsqrt(mean + EPSILON) * gain_ref[:, columns]
            column = lax.broadcasted_iota(jnp.int32, (1, 128), 1) + begin
            plain = (core == 1) & (column < YW)
            result = jnp.where(plain, value, scaled).astype(BF16)
            if begin + 128 <= YW:
                pairs_ref[begin // 128 * shard : begin // 128 * shard + rows, :] = result
            elif begin < YW:
                pairs_ref[2 * shard :, :HD] = result[:half, :HD]
                pairs_ref[2 * shard : shard + half + rows, HD:] = result[half:, :HD]
                queries_ref[:, :HD] = result[:, HD:]
            else:
                queries_ref[:, begin - YW : begin + 128 - YW] = result


def unpack(packed, room, part):
    shard = packed.shape[0] * 2 // YH
    half = shard // 2
    begin = part * shard
    room[0, begin : begin + shard, :] = packed[:shard, :]
    room[1, begin : begin + shard, :] = packed[shard : 2 * shard, :]
    room[2, begin : begin + half, :HD] = packed[2 * shard :, :HD]
    room[2, begin + half : begin + shard, :HD] = packed[2 * shard :, HD:]


def attend_kernel(counts_ref, own, beside, own_q, beside_q, far, far_beside, out_ref, keys, values):
    core, z0 = lax.axis_index("core"), lax.axis_index("z0")
    text_valid = counts_ref[lax.axis_index("x") * 4 + lax.axis_index("z1")]
    shard = own.shape[0] * 2 // YH
    rows = out_ref.shape[0] * 2 // YH
    image = shard - 8 * TEXT_ROWS
    for part, (mine, other) in enumerate(((own, beside), (far, far_beside))):

        @pl.when(core == 0)
        def _():
            unpack(mine, keys, part)
            unpack(other, values, part)

        @pl.when(core == 1)
        def _():
            unpack(other, keys, part)
            unpack(mine, values, part)

    column = lax.broadcasted_iota(jnp.int32, (1, 2 * shard), 1)
    is_far = column >= shard
    column = jnp.where(is_far, column - shard, column)
    slot = column - image + 8 * TEXT_ROWS * jnp.where(is_far, 1 - z0, z0)
    bias = jnp.where((column < image) | (slot < text_valid), 0.0, MASKED).astype(F32)
    split = HALF - YW
    each = rows // 4
    half = rows // 2
    places = [pl.ds(pl.multiple_of((2 * y + core) * each, 16), each) for y in range(4)]
    mine, other = (
        jnp.concatenate([ref[at, :] for at in places], 0) for ref in (own_q, beside_q)
    )
    first = jnp.where(core == 0, mine, other)
    second = jnp.where(core == 0, other, mine)
    for head in range(YH):
        columns = slice(head * HD, (head + 1) * HD)
        lanes = head % 2 * HD
        if head * HD < split:
            queries = first[:, columns]
        else:
            queries = second[:, head * HD - split : (head + 1) * HD - split]
        scores = lax.dot_general(
            queries * BF16(HD**-0.5),
            keys[head // 2, :, lanes : lanes + HD],
            (((1,), (1,)), ((), ())),
            preferred_element_type=F32,
        )
        scores = scores + bias
        peak = jnp.max(scores, axis=-1, keepdims=True)
        weights = jnp.exp(scores - peak)
        totals = jnp.sum(weights, axis=-1, keepdims=True)
        mixed = jnp.dot(
            weights.astype(BF16),
            values[head // 2, :, lanes : lanes + HD],
            preferred_element_type=F32,
        )
        attended = (mixed / totals).astype(BF16)
        at = head // 2 * rows
        if head < YH - 1:
            out_ref[at : at + rows, lanes : lanes + HD] = attended
        else:
            out_ref[at : at + half, :HD] = attended[:half]
            out_ref[at : at + half, HD:] = attended[half:]


def arrange_kernel(gathered_ref, out_ref, weights):
    each = weights.shape[0] // 32
    gap = gathered_ref.shape[0] // 16
    for place in range(16):
        value = gathered_ref[place * gap : (place + 1) * gap, :].astype(F32)
        core, z = divmod(place, 8)
        for x in range(2):
            at = ((x * 8 + z) * 2 + core) * each
            weights[at : at + each, :] = value[x * each : (x + 1) * each]
    out_ref[...] = weights[...].astype(BF16)


def finish_kernel(a0, a1, a2, a3, weight_ref, o0, o1, o2, o3, heads, result):
    y = lax.axis_index("y")
    rows = a0.shape[0] * 2 // YH
    half = rows // 2
    for by, attended in enumerate((a0, a1, a2, a3)):
        place = lax.rem(y + 4 - by, 4)
        heads[place, :, :128] = attended[:rows, :]
        heads[place, :, 128:256] = attended[rows : 2 * rows, :]
        heads[place, :half, 256:YW] = attended[2 * rows :, :HD]
        heads[place, half:, 256:YW] = attended[2 * rows :, HD:]
    total = None
    for q in range(4):
        size = min(YW, HEADS * HD - q * YW)
        part = lax.dot_general(
            heads[q][:, :size],
            weight_ref[:, q * YW : q * YW + size],
            (((1,), (1,)), ((), ())),
            preferred_element_type=F32,
        )
        total = part if total is None else total + part
    rows = o0.shape[0]
    result[...] = total.astype(BF16).reshape(4, rows, total.shape[1])
    for by, out_ref in enumerate((o0, o1, o2, o3)):
        out_ref[...] = result[lax.rem(y + by, 4)]


def assemble_kernel(modulation, raw_ref, n0, n1, n2, n3, out_ref, branch):
    y = lax.axis_index("y")
    run = n0.shape[1] // 16
    for by, part in enumerate((n0, n1, n2, n3)):
        value = part[...].astype(F32)
        for q in range(4):

            @pl.when(lax.rem(y + 4 - by, 4) == q)
            def _():
                for m in range(16):
                    at = (m * 4 + q) * run
                    branch[:, at : at + run] = value[:, m * run : (m + 1) * run]

    out_ref[...] = (raw_ref[...].astype(F32) + modulation[2] * branch[...]).astype(BF16)


def in_vmem(kernel, out_shape, args, flops=0, scratch=(), scalars=0, after=(), anywhere=(), limit=8):
    size = sum(a.size * a.dtype.itemsize for a in args)
    vmem = pl.BlockSpec(memory_space=pltpu.VMEM)
    return pl.pallas_call(
        kernel,
        out_shape=out_shape,
        in_specs=[pl.BlockSpec(memory_space=pltpu.SMEM)] * scalars
        + [vmem] * (len(args) - scalars)
        + [pl.BlockSpec(memory_space=pl.ANY)] * len(anywhere)
        + [vmem] * len(after),
        out_specs=jax.tree.map(lambda _: vmem, out_shape),
        scratch_shapes=list(scratch),
        compiler_params=pltpu.CompilerParams(vmem_limit_bytes=limit * 1024 * 1024),
        cost_estimate=pl.CostEstimate(flops=flops, bytes_accessed=size, transcendentals=0),
    )(*args, *anywhere, *after)


def per_device(
    stale_states, mod_table, timesteps, text_count, text_kv, qkv_weight, out_weight, qk_gain
):
    rows, width = stale_states.shape[1:]
    head_width = HEADS * HD
    weight_rows = qkv_weight.shape[1]
    quarter = width // 4
    split = HALF - YW

    halves, modulation = in_vmem(
        prepare_kernel,
        (jax.ShapeDtypeStruct((8, 24, HALF), BF16), jax.ShapeDtypeStruct((3, 1, width), F32)),
        (timesteps, qkv_weight[0], text_kv),
        scratch=[pltpu.VMEM((8, 24, HALF), F32), pltpu.SemaphoreType.DMA],
        scalars=1,
        anywhere=(mod_table.reshape(mod_table.shape[1:3] + (1, width)),),
        limit=60,
    )
    received = lax.all_to_all(halves, ("y", "core"), split_axis=0, concat_axis=0, tiled=True)
    shard = jnp.transpose(out_weight[0])

    raw = permuted(stale_states[0], "comp", 1)
    h = in_vmem(
        modulate_kernel, jax.ShapeDtypeStruct((rows, 16 * SLOT), BF16), (modulation, raw)
    )
    block, text = in_vmem(
        compact_kernel,
        (
            jax.ShapeDtypeStruct((CHUNK, HALF), BF16),
            jax.ShapeDtypeStruct((8 * TEXT_ROWS, YW), BF16),
        ),
        (received,),
        flops=7 * 10**10,
        scratch=[pltpu.VMEM((CHUNK, HALF), F32), pltpu.VMEM((8 * TEXT_ROWS, YW), F32)],
        after=(h,),
    )
    h = lax.all_gather(h, ("y", "core"), axis=0, tiled=True)

    ahead = lambda part: permuted(part, Z, 1)
    behind = lambda part: permuted(part, Z, 7)
    other = permuted(block, "x", 1)
    own_aheads, own_behinds = [ahead(block)], [behind(block)]
    other_aheads, other_behinds = [ahead(other)], [behind(other)]
    for step in range(2, 5):
        own_aheads.append(ahead(own_aheads[-1]))
        other_behinds.append(behind(other_behinds[-1]))
        if step < 4:
            own_behinds.append(behind(own_behinds[-1]))
            other_aheads.append(ahead(other_aheads[-1]))
    blocks = [block, other]
    for step in range(1, 5):
        blocks += [own_aheads[step - 1], other_behinds[step - 1]]
        if step < 4:
            blocks += [own_behinds[step - 1], other_aheads[step - 1]]

    shard_beside = permuted(hold(shard, block), "x", 1)
    both = in_vmem(
        beside_kernel,
        jax.ShapeDtypeStruct((40, head_width), BF16),
        (shard, shard_beside),
        scratch=[pltpu.VMEM((40, head_width), F32)],
        after=(own_aheads[1], own_behinds[1], other_aheads[0], other_behinds[0]),
    )
    out_columns = lax.all_gather(both, ("core", "z1", "z0"), axis=0, tiled=True)

    shard_rows = 8 * (rows + TEXT_ROWS)
    pairs, queries = in_vmem(
        project_kernel,
        (
            jax.ShapeDtypeStruct((shard_rows // 2 * YH, 128), BF16),
            jax.ShapeDtypeStruct((8 * rows, split), BF16),
        ),
        (qk_gain[0], h, text, *blocks),
        flops=2 * 8 * rows * 16 * SLOT * HALF,
        scratch=[
            pltpu.VMEM((16, SLOT, HALF), BF16),
            pltpu.VMEM((1, HALF), F32),
        ],
    )

    far = permuted(pairs, "z0", 1)
    attended = in_vmem(
        attend_kernel,
        jax.ShapeDtypeStruct((2 * rows * YH, 128), BF16),
        (
            text_count,
            pairs,
            permuted(pairs, "core", 1),
            queries,
            permuted(queries, "core", 1),
            far,
            permuted(far, "core", 1),
        ),
        flops=4 * 4 * rows * 2 * shard_rows * YW,
        scratch=[pltpu.VMEM((3, 2 * shard_rows, 128), BF16)] * 2,
        scalars=1,
    )

    out_columns = in_vmem(
        arrange_kernel,
        jax.ShapeDtypeStruct((32 * weight_rows, head_width), BF16),
        (out_columns,),
        flops=10**10,
        scratch=[pltpu.VMEM((32 * weight_rows, head_width), F32)],
    )
    gathered = tuple(permuted(attended, "y", by) for by in (1, 2, 3))
    parts = in_vmem(
        finish_kernel,
        (jax.ShapeDtypeStruct((rows, quarter), BF16),) * 4,
        (attended,)
        + gathered
        + (out_columns,),
        flops=2 * 4 * rows * head_width * quarter,
        scratch=[
            pltpu.VMEM((4, 4 * rows, YW), BF16),
            pltpu.VMEM((4, rows, quarter), BF16),
        ],
    )
    parts = [parts[0]] + [permuted(parts[by], "y", by) for by in (1, 2, 3)]
    new = in_vmem(
        assemble_kernel,
        jax.ShapeDtypeStruct((rows, width), BF16),
        (modulation, raw, *parts),
        scratch=[pltpu.VMEM((rows, width), F32)],
    )
    return new[None]


def solution(mesh):
    fine = Mesh(np.asarray(mesh.devices).reshape(SIZES), AXES)
    in_specs = (
        P("comp", SEQ, None),
        P("comp", None, None, None),
        P(),
        P(),
        P(None, SEQ, None),
        P("comp", SEQ, None),
        P("comp", None, SEQ),
        P("comp", None, None),
    )
    return jax.shard_map(
        per_device, mesh=fine, in_specs=in_specs, out_specs=P("comp", SEQ, None), check_vma=False
    )
```

```python
import jax
import jax.numpy as jnp
import numpy as np
from jax import lax
from jax.experimental import pallas as pl
from jax.experimental.pallas import tpu as pltpu
from jax.sharding import Mesh
from jax.sharding import PartitionSpec as P

AXES = ("comp", "x", "z1", "z0", "y", "core")
SIZES = (2, 2, 4, 2, 4, 2)
SEQ = AXES[1:]
Z = ("z1", "z0")
HEADS = 19
HD = 64
YH = 5
YW = YH * HD
HALF = 512
TEXT_ROWS = 8
CHUNK = 152
SLOT = 160
EPSILON = 1e-06
MASKED = -1e30
BF16 = jnp.bfloat16
F32 = jnp.float32


def permuted(array, axis, by):
    devices = lax.axis_size(axis)
    return lax.ppermute(array, axis, [(i, (i + by) % devices) for i in range(devices)])


def hold_kernel(array_ref, after_ref, out_ref):
    out_ref[...] = array_ref[...]


def hold(array, after):
    return in_vmem(
        hold_kernel, jax.ShapeDtypeStruct(array.shape, array.dtype), (array,), after=(after,)
    )


def beside_kernel(mine_ref, other_ref, *refs):
    out_ref, room = refs[-2:]
    x = lax.axis_index("x")
    used = mine_ref.shape[0]
    room[...] = jnp.zeros_like(room)
    mine, other = mine_ref[...].astype(F32), other_ref[...].astype(F32)
    room[:used, :] = jnp.where(x == 0, mine, other)
    room[used : 2 * used, :] = jnp.where(x == 0, other, mine)
    out_ref[...] = room[...].astype(BF16)


def prepare_kernel(steps_ref, weight_ref, text_ref, table_ref, out_ref, picked_ref, room, arrived):
    step = steps_ref[lax.axis_index("x") * 4 + lax.axis_index("z1")]
    copy = pltpu.make_async_copy(table_ref.at[step], picked_ref, arrived)
    copy.start()
    weight_rows = weight_ref.shape[0]
    head_width = HEADS * HD
    room[...] = jnp.zeros_like(room)
    for y in range(4):
        first = y * YW
        split = HALF - YW
        for core in range(2):
            slot = y * 2 + core
            base = (core + 1) * head_width
            size = min(YW, head_width - first)
            room[slot, :weight_rows, :size] = weight_ref[:, base + first : base + first + size].astype(F32)
            begin = first + core * split
            query_size = min(YW - split if core else split, head_width - begin)
            room[slot, :weight_rows, YW : YW + query_size] = weight_ref[
                :, begin : begin + query_size
            ].astype(F32)
            text = text_ref[core, :, first : first + size].astype(F32)
            room[slot, 19:24, :size] = text[:5]
            room[slot, 19:22, YW:] = text[5:8, :split]
            if size > split:
                room[slot, 22:23, YW : YW + size - split] = text[5:6, split:size]
                room[slot, 23:24, YW : YW + size - split] = text[6:7, split:size]
                room[slot, 22:23, YW + 128 :] = text[7:8, split : split + 64]
            if size == YW:
                room[slot, 23:24, YW + 128 :] = text[7:8, split + 64 :]
    out_ref[...] = room[...].astype(BF16)
    copy.wait()


def compact_kernel(received_ref, *refs):
    block_ref, text_ref, rows_room, text_room = refs[-4:]
    split = HALF - YW
    for source in range(8):
        value = received_ref[source].astype(F32)
        rows_room[source * 19 : (source + 1) * 19, :] = value[:19]
        at = source * TEXT_ROWS
        text_room[at : at + 5, :] = value[19:24, :YW]
        text_room[at + 5 : at + 8, :split] = value[19:22, YW:]
        text_room[at + 5 : at + 6, split:] = value[22:23, YW : YW + 128]
        text_room[at + 6 : at + 7, split:] = value[23:24, YW : YW + 128]
        text_room[at + 7 : at + 8, split : split + 64] = value[22:23, YW + 128 :]
        text_room[at + 7 : at + 8, split + 64 :] = value[23:24, YW + 128 :]
    block_ref[...] = rows_room[...].astype(BF16)
    text_ref[...] = text_room[...].astype(BF16)


def modulate_kernel(modulation, raw_ref, h_ref):
    h_ref[...] = jnp.zeros_like(h_ref)
    rows = raw_ref.shape[0] // 8
    for part in range(8):
        at = slice(part * rows, (part + 1) * rows)
        wide = raw_ref[at, :].astype(F32)
        centred = wide - jnp.mean(wide, axis=-1, keepdims=True)
        square = jnp.mean(centred * centred, axis=-1, keepdims=True)
        normed = centred * lax.rsqrt(square + EPSILON)
        modulated = normed * (1.0 + modulation[1]) + modulation[0]
        modulated = modulated.astype(BF16)
        for slot in range(16):
            h_ref[at, slot * SLOT : slot * SLOT + CHUNK] = modulated[
                :, slot * CHUNK : (slot + 1) * CHUNK
            ]


def places_of_blocks():
    x = lax.axis_index("x")
    z = lax.axis_index("z1") * 2 + lax.axis_index("z0")
    slots = [x * 8 + z, (1 - x) * 8 + z]
    for step in range(1, 5):
        slots += [x * 8 + lax.rem(z + 8 - step, 8), (1 - x) * 8 + lax.rem(z + step, 8)]
        if step < 4:
            slots += [x * 8 + lax.rem(z + step, 8), (1 - x) * 8 + lax.rem(z + 8 - step, 8)]
    return slots


def project_kernel(gains_ref, h_ref, text_ref, *refs):
    blocks, (pairs_ref, queries_ref, whole, gain_ref) = refs[:16], refs[16:]
    y, core = lax.axis_index("y"), lax.axis_index("core")
    split = HALF - YW
    gain_ref[...] = jnp.ones_like(gain_ref)
    for at in range(4):
        first = at * YW
        size = min(YW, HEADS * HD - first)

        @pl.when((y == at) & (core == 0))
        def _():
            gain_ref[:, :size] = gains_ref[1:2, first : first + size]
            gain_ref[:, YW:] = gains_ref[0:1, first : first + split]

        @pl.when((y == at) & (core == 1))
        def _():
            gain_ref[:, YW : YW + size - split] = gains_ref[0:1, first + split : first + size]

    whole[:, CHUNK:, :] = jnp.zeros((16, SLOT - CHUNK, HALF), BF16)
    for slot, block in zip(places_of_blocks(), blocks):
        whole[slot, :CHUNK, :] = block[...]
    rows = h_ref.shape[0]
    shard = pairs_ref.shape[0] * 2 // YH
    half = shard // 2
    pairs_ref[rows:shard, :] = text_ref[:, :128]
    pairs_ref[shard + rows : 2 * shard, :] = text_ref[:, 128:256]
    pairs_ref[shard + half + rows :, HD:] = text_ref[:, 256:]
    low = lax.broadcasted_iota(jnp.int32, (rows, 128), 1) < HD
    for tile in range(0, HALF, 256):
        weights = whole[:, :, tile : tile + 256].reshape(16 * SLOT, 256)
        product = jnp.dot(h_ref[...], weights, preferred_element_type=F32)
        for part in range(2):
            begin = tile + part * 128
            columns = slice(begin, begin + 128)
            value = product[:, part * 128 : part * 128 + 128]
            square = value * value
            low_sum = jnp.sum(jnp.where(low, square, 0.0), axis=-1, keepdims=True)
            high_sum = jnp.sum(jnp.where(low, 0.0, square), axis=-1, keepdims=True)
            mean = jnp.where(low, low_sum, high_sum) * (1.0 / HD)
            scaled = value * lax.rsqrt(mean + EPSILON) * gain_ref[:, columns]
            column = lax.broadcasted_iota(jnp.int32, (1, 128), 1) + begin
            plain = (core == 1) & (column < YW)
            result = jnp.where(plain, value, scaled).astype(BF16)
            if begin + 128 <= YW:
                pairs_ref[begin // 128 * shard : begin // 128 * shard + rows, :] = result
            elif begin < YW:
                pairs_ref[2 * shard :, :HD] = result[:half, :HD]
                pairs_ref[2 * shard : shard + half + rows, HD:] = result[half:, :HD]
                queries_ref[:, :HD] = result[:, HD:]
            else:
                queries_ref[:, begin - YW : begin + 128 - YW] = result


def unpack(packed, room, part):
    shard = packed.shape[0] * 2 // YH
    half = shard // 2
    begin = part * shard
    room[0, begin : begin + shard, :] = packed[:shard, :]
    room[1, begin : begin + shard, :] = packed[shard : 2 * shard, :]
    room[2, begin : begin + half, :HD] = packed[2 * shard :, :HD]
    room[2, begin + half : begin + shard, :HD] = packed[2 * shard :, HD:]


def attend_kernel(counts_ref, own, beside, own_q, beside_q, far, far_beside, out_ref, keys, values):
    core, z0 = lax.axis_index("core"), lax.axis_index("z0")
    text_valid = counts_ref[lax.axis_index("x") * 4 + lax.axis_index("z1")]
    shard = own.shape[0] * 2 // YH
    rows = out_ref.shape[0] * 2 // YH
    image = shard - 8 * TEXT_ROWS
    for part, (mine, other) in enumerate(((own, beside), (far, far_beside))):

        @pl.when(core == 0)
        def _():
            unpack(mine, keys, part)
            unpack(other, values, part)

        @pl.when(core == 1)
        def _():
            unpack(other, keys, part)
            unpack(mine, values, part)

    column = lax.broadcasted_iota(jnp.int32, (1, 2 * shard), 1)
    is_far = column >= shard
    column = jnp.where(is_far, column - shard, column)
    slot = column - image + 8 * TEXT_ROWS * jnp.where(is_far, 1 - z0, z0)
    bias = jnp.where((column < image) | (slot < text_valid), 0.0, MASKED).astype(F32)
    split = HALF - YW
    each = rows // 4
    half = rows // 2
    places = [pl.ds(pl.multiple_of((2 * y + core) * each, 16), each) for y in range(4)]
    mine, other = (
        jnp.concatenate([ref[at, :] for at in places], 0) for ref in (own_q, beside_q)
    )
    first = jnp.where(core == 0, mine, other)
    second = jnp.where(core == 0, other, mine)
    for head in range(YH):
        columns = slice(head * HD, (head + 1) * HD)
        lanes = head % 2 * HD
        if head * HD < split:
            queries = first[:, columns]
        else:
            queries = second[:, head * HD - split : (head + 1) * HD - split]
        scores = lax.dot_general(
            queries * BF16(HD**-0.5),
            keys[head // 2, :, lanes : lanes + HD],
            (((1,), (1,)), ((), ())),
            preferred_element_type=F32,
        )
        scores = scores + bias
        peak = jnp.max(scores, axis=-1, keepdims=True)
        weights = jnp.exp(scores - peak)
        totals = jnp.sum(weights, axis=-1, keepdims=True)
        mixed = jnp.dot(
            weights.astype(BF16),
            values[head // 2, :, lanes : lanes + HD],
            preferred_element_type=F32,
        )
        attended = (mixed / totals).astype(BF16)
        at = head // 2 * rows
        if head < YH - 1:
            out_ref[at : at + rows, lanes : lanes + HD] = attended
        else:
            out_ref[at : at + half, :HD] = attended[:half]
            out_ref[at : at + half, HD:] = attended[half:]


def arrange_kernel(gathered_ref, out_ref, weights):
    each = weights.shape[0] // 32
    gap = gathered_ref.shape[0] // 16
    for place in range(16):
        value = gathered_ref[place * gap : (place + 1) * gap, :].astype(F32)
        core, z = divmod(place, 8)
        for x in range(2):
            at = ((x * 8 + z) * 2 + core) * each
            weights[at : at + each, :] = value[x * each : (x + 1) * each]
    out_ref[...] = weights[...].astype(BF16)


def finish_kernel(a0, a1, a2, a3, weight_ref, o0, o1, o2, o3, heads, result):
    y = lax.axis_index("y")
    rows = a0.shape[0] * 2 // YH
    half = rows // 2
    for by, attended in enumerate((a0, a1, a2, a3)):
        place = lax.rem(y + 4 - by, 4)
        heads[place, :, :128] = attended[:rows, :]
        heads[place, :, 128:256] = attended[rows : 2 * rows, :]
        heads[place, :half, 256:YW] = attended[2 * rows :, :HD]
        heads[place, half:, 256:YW] = attended[2 * rows :, HD:]
    total = None
    for q in range(4):
        size = min(YW, HEADS * HD - q * YW)
        part = lax.dot_general(
            heads[q][:, :size],
            weight_ref[:, q * YW : q * YW + size],
            (((1,), (1,)), ((), ())),
            preferred_element_type=F32,
        )
        total = part if total is None else total + part
    rows = o0.shape[0]
    result[...] = total.astype(BF16).reshape(4, rows, total.shape[1])
    for by, out_ref in enumerate((o0, o1, o2, o3)):
        out_ref[...] = result[lax.rem(y + by, 4)]


def place_columns(part, by, branch):
    y = lax.axis_index("y")
    run = part.shape[1] // 16
    value = part[...].astype(F32)
    for q in range(4):

        @pl.when(lax.rem(y + 4 - by, 4) == q)
        def _():
            for m in range(16):
                at = (m * 4 + q) * run
                branch[:, at : at + run] = value[:, m * run : (m + 1) * run]


def assemble_early_kernel(n0, n1, n3, branch):
    for by, part in ((0, n0), (1, n1), (3, n3)):
        place_columns(part, by, branch)


def assemble_kernel(modulation, raw_ref, early_ref, n2, out_ref, branch):
    branch[...] = early_ref[...]
    place_columns(n2, 2, branch)
    out_ref[...] = (raw_ref[...].astype(F32) + modulation[2] * branch[...]).astype(BF16)


def in_vmem(kernel, out_shape, args, flops=0, scratch=(), scalars=0, after=(), anywhere=(), limit=8):
    size = sum(a.size * a.dtype.itemsize for a in args)
    vmem = pl.BlockSpec(memory_space=pltpu.VMEM)
    return pl.pallas_call(
        kernel,
        out_shape=out_shape,
        in_specs=[pl.BlockSpec(memory_space=pltpu.SMEM)] * scalars
        + [vmem] * (len(args) - scalars)
        + [pl.BlockSpec(memory_space=pl.ANY)] * len(anywhere)
        + [vmem] * len(after),
        out_specs=jax.tree.map(lambda _: vmem, out_shape),
        scratch_shapes=list(scratch),
        compiler_params=pltpu.CompilerParams(vmem_limit_bytes=limit * 1024 * 1024),
        cost_estimate=pl.CostEstimate(flops=flops, bytes_accessed=size, transcendentals=0),
    )(*args, *anywhere, *after)


def per_device(
    stale_states, mod_table, timesteps, text_count, text_kv, qkv_weight, out_weight, qk_gain
):
    rows, width = stale_states.shape[1:]
    head_width = HEADS * HD
    weight_rows = qkv_weight.shape[1]
    quarter = width // 4
    split = HALF - YW

    halves, modulation = in_vmem(
        prepare_kernel,
        (jax.ShapeDtypeStruct((8, 24, HALF), BF16), jax.ShapeDtypeStruct((3, 1, width), F32)),
        (timesteps, qkv_weight[0], text_kv),
        scratch=[pltpu.VMEM((8, 24, HALF), F32), pltpu.SemaphoreType.DMA],
        scalars=1,
        anywhere=(mod_table.reshape(mod_table.shape[1:3] + (1, width)),),
        limit=60,
    )
    received = lax.all_to_all(halves, ("y", "core"), split_axis=0, concat_axis=0, tiled=True)
    shard = jnp.transpose(out_weight[0])

    raw = permuted(stale_states[0], "comp", 1)
    block, text = in_vmem(
        compact_kernel,
        (
            jax.ShapeDtypeStruct((CHUNK, HALF), BF16),
            jax.ShapeDtypeStruct((8 * TEXT_ROWS, YW), BF16),
        ),
        (received,),
        flops=35 * 10**9,
        scratch=[pltpu.VMEM((CHUNK, HALF), F32), pltpu.VMEM((8 * TEXT_ROWS, YW), F32)],
        after=(raw,),
    )
    h = in_vmem(
        modulate_kernel,
        jax.ShapeDtypeStruct((8 * rows, 16 * SLOT), BF16),
        (modulation, lax.all_gather(raw, ("y", "core"), axis=0, tiled=True)),
        flops=2 * 10**10,
    )

    ahead = lambda part: permuted(part, Z, 1)
    behind = lambda part: permuted(part, Z, 7)
    other = permuted(block, "x", 1)
    own_aheads, own_behinds = [ahead(block)], [behind(block)]
    other_aheads, other_behinds = [ahead(other)], [behind(other)]
    for step in range(2, 5):
        own_aheads.append(ahead(own_aheads[-1]))
        other_behinds.append(behind(other_behinds[-1]))
        if step < 4:
            own_behinds.append(behind(own_behinds[-1]))
            other_aheads.append(ahead(other_aheads[-1]))
    blocks = [block, other]
    for step in range(1, 5):
        blocks += [own_aheads[step - 1], other_behinds[step - 1]]
        if step < 4:
            blocks += [own_behinds[step - 1], other_aheads[step - 1]]

    shard_beside = permuted(hold(shard, block), "x", 1)
    both = in_vmem(
        beside_kernel,
        jax.ShapeDtypeStruct((40, head_width), BF16),
        (shard, shard_beside),
        scratch=[pltpu.VMEM((40, head_width), F32)],
        after=(own_aheads[1], own_behinds[1], other_aheads[0], other_behinds[0]),
    )
    out_columns = lax.all_gather(both, ("core", "z1", "z0"), axis=0, tiled=True)

    shard_rows = 8 * (rows + TEXT_ROWS)
    pairs, queries = in_vmem(
        project_kernel,
        (
            jax.ShapeDtypeStruct((shard_rows // 2 * YH, 128), BF16),
            jax.ShapeDtypeStruct((8 * rows, split), BF16),
        ),
        (qk_gain[0], h, text, *blocks),
        flops=2 * 8 * rows * 16 * SLOT * HALF,
        scratch=[
            pltpu.VMEM((16, SLOT, HALF), BF16),
            pltpu.VMEM((1, HALF), F32),
        ],
    )

    far = permuted(pairs, "z0", 1)
    attended = in_vmem(
        attend_kernel,
        jax.ShapeDtypeStruct((2 * rows * YH, 128), BF16),
        (
            text_count,
            pairs,
            permuted(pairs, "core", 1),
            queries,
            permuted(queries, "core", 1),
            far,
            permuted(far, "core", 1),
        ),
        flops=4 * 4 * rows * 2 * shard_rows * YW,
        scratch=[pltpu.VMEM((3, 2 * shard_rows, 128), BF16)] * 2,
        scalars=1,
    )

    out_columns = in_vmem(
        arrange_kernel,
        jax.ShapeDtypeStruct((32 * weight_rows, head_width), BF16),
        (out_columns,),
        flops=10**10,
        scratch=[pltpu.VMEM((32 * weight_rows, head_width), F32)],
    )
    gathered = tuple(permuted(attended, "y", by) for by in (1, 2, 3))
    parts = in_vmem(
        finish_kernel,
        (jax.ShapeDtypeStruct((rows, quarter), BF16),) * 4,
        (attended,)
        + gathered
        + (out_columns,),
        flops=2 * 4 * rows * head_width * quarter,
        scratch=[
            pltpu.VMEM((4, 4 * rows, YW), BF16),
            pltpu.VMEM((4, rows, quarter), BF16),
        ],
    )
    parts = [parts[0]] + [permuted(parts[by], "y", by) for by in (1, 2, 3)]
    early = in_vmem(
        assemble_early_kernel,
        jax.ShapeDtypeStruct((rows, width), F32),
        (parts[0], parts[1], parts[3]),
        flops=10**10,
    )
    new = in_vmem(
        assemble_kernel,
        jax.ShapeDtypeStruct((rows, width), BF16),
        (modulation, raw, early, parts[2]),
        scratch=[pltpu.VMEM((rows, width), F32)],
    )
    return new[None]


def solution(mesh):
    fine = Mesh(np.asarray(mesh.devices).reshape(SIZES), AXES)
    in_specs = (
        P("comp", SEQ, None),
        P("comp", None, None, None),
        P(),
        P(),
        P(None, SEQ, None),
        P("comp", SEQ, None),
        P("comp", None, SEQ),
        P("comp", None, None),
    )
    return jax.shard_map(
        per_device, mesh=fine, in_specs=in_specs, out_specs=P("comp", SEQ, None), check_vma=False
    )
```

```python
import jax
import jax.numpy as jnp
import numpy as np
from jax import lax
from jax.experimental import pallas as pl
from jax.experimental.pallas import tpu as pltpu
from jax.sharding import Mesh
from jax.sharding import PartitionSpec as P

AXES = ("comp", "x", "z1", "z0", "y", "core")
SIZES = (2, 2, 4, 2, 4, 2)
SEQ = AXES[1:]
Z = ("z1", "z0")
HEADS = 19
HD = 64
YH = 5
YW = YH * HD
HALF = 512
TEXT_ROWS = 8
CHUNK = 152
SLOT = 160
EPSILON = 1e-06
MASKED = -1e30
BF16 = jnp.bfloat16
F32 = jnp.float32


def permuted(array, axis, by):
    devices = lax.axis_size(axis)
    return lax.ppermute(array, axis, [(i, (i + by) % devices) for i in range(devices)])


def hold_kernel(array_ref, after_ref, out_ref):
    out_ref[...] = array_ref[...]


def hold(array, after):
    return in_vmem(
        hold_kernel, jax.ShapeDtypeStruct(array.shape, array.dtype), (array,), after=(after,)
    )


def beside_kernel(mine_ref, other_ref, *refs):
    out_ref, room = refs[-2:]
    x = lax.axis_index("x")
    used = mine_ref.shape[0]
    room[...] = jnp.zeros_like(room)
    mine, other = mine_ref[...].astype(F32), other_ref[...].astype(F32)
    room[:used, :] = jnp.where(x == 0, mine, other)
    room[used : 2 * used, :] = jnp.where(x == 0, other, mine)
    out_ref[...] = room[...].astype(BF16)


def prepare_kernel(steps_ref, weight_ref, text_ref, table_ref, out_ref, picked_ref, room, arrived):
    step = steps_ref[lax.axis_index("x") * 4 + lax.axis_index("z1")]
    copy = pltpu.make_async_copy(table_ref.at[step], picked_ref, arrived)
    copy.start()
    weight_rows = weight_ref.shape[0]
    head_width = HEADS * HD
    room[...] = jnp.zeros_like(room)
    for y in range(4):
        first = y * YW
        split = HALF - YW
        for core in range(2):
            slot = y * 2 + core
            base = (core + 1) * head_width
            size = min(YW, head_width - first)
            room[slot, :weight_rows, :size] = weight_ref[:, base + first : base + first + size].astype(F32)
            begin = first + core * split
            query_size = min(YW - split if core else split, head_width - begin)
            room[slot, :weight_rows, YW : YW + query_size] = weight_ref[
                :, begin : begin + query_size
            ].astype(F32)
            text = text_ref[core, :, first : first + size].astype(F32)
            room[slot, 19:24, :size] = text[:5]
            room[slot, 19:22, YW:] = text[5:8, :split]
            if size > split:
                room[slot, 22:23, YW : YW + size - split] = text[5:6, split:size]
                room[slot, 23:24, YW : YW + size - split] = text[6:7, split:size]
                room[slot, 22:23, YW + 128 :] = text[7:8, split : split + 64]
            if size == YW:
                room[slot, 23:24, YW + 128 :] = text[7:8, split + 64 :]
    out_ref[...] = room[...].astype(BF16)
    copy.wait()


def compact_kernel(received_ref, *refs):
    block_ref, text_ref, rows_room, text_room = refs[-4:]
    split = HALF - YW
    for source in range(8):
        value = received_ref[source].astype(F32)
        rows_room[source * 19 : (source + 1) * 19, :] = value[:19]
        at = source * TEXT_ROWS
        text_room[at : at + 5, :] = value[19:24, :YW]
        text_room[at + 5 : at + 8, :split] = value[19:22, YW:]
        text_room[at + 5 : at + 6, split:] = value[22:23, YW : YW + 128]
        text_room[at + 6 : at + 7, split:] = value[23:24, YW : YW + 128]
        text_room[at + 7 : at + 8, split : split + 64] = value[22:23, YW + 128 :]
        text_room[at + 7 : at + 8, split + 64 :] = value[23:24, YW + 128 :]
    block_ref[...] = rows_room[...].astype(BF16)
    text_ref[...] = text_room[...].astype(BF16)


def modulate_kernel(modulation, raw_ref, h_ref):
    h_ref[...] = jnp.zeros_like(h_ref)
    rows = raw_ref.shape[0] // 8
    for part in range(8):
        at = slice(part * rows, (part + 1) * rows)
        wide = raw_ref[at, :].astype(F32)
        centred = wide - jnp.mean(wide, axis=-1, keepdims=True)
        square = jnp.mean(centred * centred, axis=-1, keepdims=True)
        normed = centred * lax.rsqrt(square + EPSILON)
        modulated = normed * (1.0 + modulation[1]) + modulation[0]
        modulated = modulated.astype(BF16)
        for slot in range(16):
            h_ref[at, slot * SLOT : slot * SLOT + CHUNK] = modulated[
                :, slot * CHUNK : (slot + 1) * CHUNK
            ]


def places_of_blocks():
    x = lax.axis_index("x")
    z = lax.axis_index("z1") * 2 + lax.axis_index("z0")
    slots = [x * 8 + z, (1 - x) * 8 + z]
    for step in range(1, 5):
        slots += [x * 8 + lax.rem(z + 8 - step, 8), (1 - x) * 8 + lax.rem(z + step, 8)]
        if step < 4:
            slots += [x * 8 + lax.rem(z + step, 8), (1 - x) * 8 + lax.rem(z + 8 - step, 8)]
    return slots


def project_kernel(gains_ref, h_ref, text_ref, *refs):
    blocks, (pairs_ref, queries_ref, whole, gain_ref) = refs[:16], refs[16:]
    y, core = lax.axis_index("y"), lax.axis_index("core")
    split = HALF - YW
    gain_ref[...] = jnp.ones_like(gain_ref)
    for at in range(4):
        first = at * YW
        size = min(YW, HEADS * HD - first)

        @pl.when((y == at) & (core == 0))
        def _():
            gain_ref[:, :size] = gains_ref[1:2, first : first + size]
            gain_ref[:, YW:] = gains_ref[0:1, first : first + split]

        @pl.when((y == at) & (core == 1))
        def _():
            gain_ref[:, YW : YW + size - split] = gains_ref[0:1, first + split : first + size]

    whole[:, CHUNK:, :] = jnp.zeros((16, SLOT - CHUNK, HALF), BF16)
    for slot, block in zip(places_of_blocks(), blocks):
        whole[slot, :CHUNK, :] = block[...]
    rows = h_ref.shape[0]
    shard = pairs_ref.shape[0] * 2 // YH
    half = shard // 2
    pairs_ref[rows:shard, :] = text_ref[:, :128]
    pairs_ref[shard + rows : 2 * shard, :] = text_ref[:, 128:256]
    pairs_ref[shard + half + rows :, HD:] = text_ref[:, 256:]
    low = lax.broadcasted_iota(jnp.int32, (rows, 128), 1) < HD
    for tile in range(0, HALF, 256):
        weights = whole[:, :, tile : tile + 256].reshape(16 * SLOT, 256)
        product = jnp.dot(h_ref[...], weights, preferred_element_type=F32)
        for part in range(2):
            begin = tile + part * 128
            columns = slice(begin, begin + 128)
            value = product[:, part * 128 : part * 128 + 128]
            square = value * value
            low_sum = jnp.sum(jnp.where(low, square, 0.0), axis=-1, keepdims=True)
            high_sum = jnp.sum(jnp.where(low, 0.0, square), axis=-1, keepdims=True)
            mean = jnp.where(low, low_sum, high_sum) * (1.0 / HD)
            scaled = value * lax.rsqrt(mean + EPSILON) * gain_ref[:, columns]
            column = lax.broadcasted_iota(jnp.int32, (1, 128), 1) + begin
            plain = (core == 1) & (column < YW)
            result = jnp.where(plain, value, scaled).astype(BF16)
            if begin + 128 <= YW:
                pairs_ref[begin // 128 * shard : begin // 128 * shard + rows, :] = result
            elif begin < YW:
                pairs_ref[2 * shard :, :HD] = result[:half, :HD]
                pairs_ref[2 * shard : shard + half + rows, HD:] = result[half:, :HD]
                queries_ref[:, :HD] = result[:, HD:]
            else:
                queries_ref[:, begin - YW : begin + 128 - YW] = result


def unpack(packed, room, part):
    shard = packed.shape[0] * 2 // YH
    half = shard // 2
    begin = part * shard
    room[0, begin : begin + shard, :] = packed[:shard, :]
    room[1, begin : begin + shard, :] = packed[shard : 2 * shard, :]
    room[2, begin : begin + half, :HD] = packed[2 * shard :, :HD]
    room[2, begin + half : begin + shard, :HD] = packed[2 * shard :, HD:]


def attend_kernel(counts_ref, own, beside, own_q, beside_q, far, far_beside, out_ref, keys, values):
    core, z0 = lax.axis_index("core"), lax.axis_index("z0")
    text_valid = counts_ref[lax.axis_index("x") * 4 + lax.axis_index("z1")]
    shard = own.shape[0] * 2 // YH
    rows = out_ref.shape[0] * 2 // YH
    image = shard - 8 * TEXT_ROWS
    for part, (mine, other) in enumerate(((own, beside), (far, far_beside))):

        @pl.when(core == 0)
        def _():
            unpack(mine, keys, part)
            unpack(other, values, part)

        @pl.when(core == 1)
        def _():
            unpack(other, keys, part)
            unpack(mine, values, part)

    column = lax.broadcasted_iota(jnp.int32, (1, 2 * shard), 1)
    is_far = column >= shard
    column = jnp.where(is_far, column - shard, column)
    slot = column - image + 8 * TEXT_ROWS * jnp.where(is_far, 1 - z0, z0)
    bias = jnp.where((column < image) | (slot < text_valid), 0.0, MASKED).astype(F32)
    split = HALF - YW
    each = rows // 4
    half = rows // 2
    places = [pl.ds(pl.multiple_of((2 * y + core) * each, 16), each) for y in range(4)]
    mine, other = (
        jnp.concatenate([ref[at, :] for at in places], 0) for ref in (own_q, beside_q)
    )
    first = jnp.where(core == 0, mine, other)
    second = jnp.where(core == 0, other, mine)
    for head in range(YH):
        columns = slice(head * HD, (head + 1) * HD)
        lanes = head % 2 * HD
        if head * HD < split:
            queries = first[:, columns]
        else:
            queries = second[:, head * HD - split : (head + 1) * HD - split]
        scores = lax.dot_general(
            queries * BF16(HD**-0.5),
            keys[head // 2, :, lanes : lanes + HD],
            (((1,), (1,)), ((), ())),
            preferred_element_type=F32,
        )
        scores = scores + bias
        peak = jnp.max(scores, axis=-1, keepdims=True)
        weights = jnp.exp(scores - peak)
        totals = jnp.sum(weights, axis=-1, keepdims=True)
        mixed = jnp.dot(
            weights.astype(BF16),
            values[head // 2, :, lanes : lanes + HD],
            preferred_element_type=F32,
        )
        attended = (mixed / totals).astype(BF16)
        at = head // 2 * rows
        if head < YH - 1:
            out_ref[at : at + rows, lanes : lanes + HD] = attended
        else:
            out_ref[at : at + half, :HD] = attended[:half]
            out_ref[at : at + half, HD:] = attended[half:]


def finish_kernel(a0, a1, a2, a3, gathered_ref, o0, o1, o2, o3, heads, result):
    y = lax.axis_index("y")
    rows = a0.shape[0] * 2 // YH
    half = rows // 2
    for by, attended in enumerate((a0, a1, a2, a3)):
        place = lax.rem(y + 4 - by, 4)
        heads[place, :, :128] = attended[:rows, :]
        heads[place, :, 128:256] = attended[rows : 2 * rows, :]
        heads[place, :half, 256:YW] = attended[2 * rows :, :HD]
        heads[place, half:, 256:YW] = attended[2 * rows :, HD:]
    total = None
    for q in range(4):
        size = min(YW, HEADS * HD - q * YW)
        part = lax.dot_general(
            heads[q][:, :size],
            gathered_ref[:, q * YW : q * YW + size],
            (((1,), (1,)), ((), ())),
            preferred_element_type=F32,
        )
        total = part if total is None else total + part
    result[...] = total.astype(BF16).reshape(4, rows // 4, total.shape[1])
    for by, out_ref in enumerate((o0, o1, o2, o3)):
        out_ref[...] = result[lax.rem(y + by, 4)]


def place_columns(part, by, branch):
    y = lax.axis_index("y")
    run = branch.shape[1] // 128
    gap = part.shape[1] // 16
    value = part[...].astype(F32)
    for q in range(4):

        @pl.when(lax.rem(y + 4 - by, 4) == q)
        def _():
            for place in range(16):
                core, z = divmod(place, 8)
                for x in range(2):
                    at = (((x * 8 + z) * 4 + q) * 2 + core) * run
                    begin = place * gap + x * run
                    branch[:, at : at + run] = value[:, begin : begin + run]


def assemble_early_kernel(n0, n1, n3, branch):
    for by, part in ((0, n0), (1, n1), (3, n3)):
        place_columns(part, by, branch)


def assemble_kernel(modulation, raw_ref, early_ref, n2, out_ref, branch):
    branch[...] = early_ref[...]
    place_columns(n2, 2, branch)
    out_ref[...] = (raw_ref[...].astype(F32) + modulation[2] * branch[...]).astype(BF16)


def in_vmem(kernel, out_shape, args, flops=0, scratch=(), scalars=0, after=(), anywhere=(), limit=8):
    size = sum(a.size * a.dtype.itemsize for a in args)
    vmem = pl.BlockSpec(memory_space=pltpu.VMEM)
    return pl.pallas_call(
        kernel,
        out_shape=out_shape,
        in_specs=[pl.BlockSpec(memory_space=pltpu.SMEM)] * scalars
        + [vmem] * (len(args) - scalars)
        + [pl.BlockSpec(memory_space=pl.ANY)] * len(anywhere)
        + [vmem] * len(after),
        out_specs=jax.tree.map(lambda _: vmem, out_shape),
        scratch_shapes=list(scratch),
        compiler_params=pltpu.CompilerParams(vmem_limit_bytes=limit * 1024 * 1024),
        cost_estimate=pl.CostEstimate(flops=flops, bytes_accessed=size, transcendentals=0),
    )(*args, *anywhere, *after)


def per_device(
    stale_states, mod_table, timesteps, text_count, text_kv, qkv_weight, out_weight, qk_gain
):
    rows, width = stale_states.shape[1:]
    head_width = HEADS * HD
    weight_rows = qkv_weight.shape[1]
    split = HALF - YW

    halves, modulation = in_vmem(
        prepare_kernel,
        (jax.ShapeDtypeStruct((8, 24, HALF), BF16), jax.ShapeDtypeStruct((3, 1, width), F32)),
        (timesteps, qkv_weight[0], text_kv),
        scratch=[pltpu.VMEM((8, 24, HALF), F32), pltpu.SemaphoreType.DMA],
        scalars=1,
        anywhere=(mod_table.reshape(mod_table.shape[1:3] + (1, width)),),
        limit=60,
    )
    received = lax.all_to_all(halves, ("y", "core"), split_axis=0, concat_axis=0, tiled=True)
    shard = jnp.transpose(out_weight[0])

    raw = permuted(stale_states[0], "comp", 1)
    block, text = in_vmem(
        compact_kernel,
        (
            jax.ShapeDtypeStruct((CHUNK, HALF), BF16),
            jax.ShapeDtypeStruct((8 * TEXT_ROWS, YW), BF16),
        ),
        (received,),
        flops=35 * 10**9,
        scratch=[pltpu.VMEM((CHUNK, HALF), F32), pltpu.VMEM((8 * TEXT_ROWS, YW), F32)],
        after=(raw,),
    )
    h = in_vmem(
        modulate_kernel,
        jax.ShapeDtypeStruct((8 * rows, 16 * SLOT), BF16),
        (modulation, lax.all_gather(raw, ("y", "core"), axis=0, tiled=True)),
        flops=2 * 10**10,
    )

    ahead = lambda part: permuted(part, Z, 1)
    behind = lambda part: permuted(part, Z, 7)
    other = permuted(block, "x", 1)
    own_aheads, own_behinds = [ahead(block)], [behind(block)]
    other_aheads, other_behinds = [ahead(other)], [behind(other)]
    for step in range(2, 5):
        own_aheads.append(ahead(own_aheads[-1]))
        other_behinds.append(behind(other_behinds[-1]))
        if step < 4:
            own_behinds.append(behind(own_behinds[-1]))
            other_aheads.append(ahead(other_aheads[-1]))
    blocks = [block, other]
    for step in range(1, 5):
        blocks += [own_aheads[step - 1], other_behinds[step - 1]]
        if step < 4:
            blocks += [own_behinds[step - 1], other_aheads[step - 1]]

    shard_beside = permuted(hold(shard, block), "x", 1)
    both = in_vmem(
        beside_kernel,
        jax.ShapeDtypeStruct((40, head_width), BF16),
        (shard, shard_beside),
        scratch=[pltpu.VMEM((40, head_width), F32)],
        after=(own_aheads[1], own_behinds[1], other_aheads[0], other_behinds[0]),
    )
    out_columns = lax.all_gather(both, ("core", "z1", "z0"), axis=0, tiled=True)

    shard_rows = 8 * (rows + TEXT_ROWS)
    pairs, queries = in_vmem(
        project_kernel,
        (
            jax.ShapeDtypeStruct((shard_rows // 2 * YH, 128), BF16),
            jax.ShapeDtypeStruct((8 * rows, split), BF16),
        ),
        (qk_gain[0], h, text, *blocks),
        flops=2 * 8 * rows * 16 * SLOT * HALF,
        scratch=[
            pltpu.VMEM((16, SLOT, HALF), BF16),
            pltpu.VMEM((1, HALF), F32),
        ],
    )

    far = permuted(pairs, "z0", 1)
    attended = in_vmem(
        attend_kernel,
        jax.ShapeDtypeStruct((2 * rows * YH, 128), BF16),
        (
            text_count,
            pairs,
            permuted(pairs, "core", 1),
            queries,
            permuted(queries, "core", 1),
            far,
            permuted(far, "core", 1),
        ),
        flops=4 * 4 * rows * 2 * shard_rows * YW,
        scratch=[pltpu.VMEM((3, 2 * shard_rows, 128), BF16)] * 2,
        scalars=1,
    )

    gathered = tuple(permuted(attended, "y", by) for by in (1, 2, 3))
    columns = out_columns.shape[0]
    parts = in_vmem(
        finish_kernel,
        (jax.ShapeDtypeStruct((rows, columns), BF16),) * 4,
        (attended,) + gathered + (out_columns,),
        flops=2 * 4 * rows * head_width * columns,
        scratch=[
            pltpu.VMEM((4, 4 * rows, YW), BF16),
            pltpu.VMEM((4, rows, columns), BF16),
        ],
    )
    parts = [parts[0]] + [permuted(parts[by], "y", by) for by in (1, 2, 3)]
    early = in_vmem(
        assemble_early_kernel,
        jax.ShapeDtypeStruct((rows, width), F32),
        (parts[0], parts[1], parts[3]),
        flops=10**10,
    )
    new = in_vmem(
        assemble_kernel,
        jax.ShapeDtypeStruct((rows, width), BF16),
        (modulation, raw, early, parts[2]),
        scratch=[pltpu.VMEM((rows, width), F32)],
    )
    return new[None]


def solution(mesh):
    fine = Mesh(np.asarray(mesh.devices).reshape(SIZES), AXES)
    in_specs = (
        P("comp", SEQ, None),
        P("comp", None, None, None),
        P(),
        P(),
        P(None, SEQ, None),
        P("comp", SEQ, None),
        P("comp", None, SEQ),
        P("comp", None, None),
    )
    return jax.shard_map(
        per_device, mesh=fine, in_specs=in_specs, out_specs=P("comp", SEQ, None), check_vma=False
    )
```

```python
import jax
import jax.numpy as jnp
import numpy as np
from jax import lax
from jax.experimental import pallas as pl
from jax.experimental.pallas import tpu as pltpu
from jax.sharding import Mesh
from jax.sharding import PartitionSpec as P

AXES = ("comp", "x", "z1", "z0", "y", "core")
SIZES = (2, 2, 4, 2, 4, 2)
SEQ = AXES[1:]
Z = ("z1", "z0")
HEADS = 19
HD = 64
YH = 5
YW = YH * HD
HALF = 512
TEXT_ROWS = 8
CHUNK = 152
SLOT = 160
EPSILON = 1e-06
MASKED = -1e30
BF16 = jnp.bfloat16
F32 = jnp.float32


def permuted(array, axis, by):
    devices = lax.axis_size(axis)
    return lax.ppermute(array, axis, [(i, (i + by) % devices) for i in range(devices)])


def hold_kernel(array_ref, after_ref, out_ref):
    out_ref[...] = array_ref[...]


def hold(array, after):
    return in_vmem(
        hold_kernel, jax.ShapeDtypeStruct(array.shape, array.dtype), (array,), after=(after,)
    )


def beside_kernel(mine_ref, other_ref, *refs):
    out_ref, room = refs[-2:]
    x = lax.axis_index("x")
    used = mine_ref.shape[0]
    room[...] = jnp.zeros_like(room)
    mine, other = mine_ref[...].astype(F32), other_ref[...].astype(F32)
    room[:used, :] = jnp.where(x == 0, mine, other)
    room[used : 2 * used, :] = jnp.where(x == 0, other, mine)
    out_ref[...] = room[...].astype(BF16)


def prepare_kernel(steps_ref, weight_ref, text_ref, table_ref, out_ref, picked_ref, room, arrived):
    step = steps_ref[lax.axis_index("x") * 4 + lax.axis_index("z1")]
    copy = pltpu.make_async_copy(table_ref.at[step], picked_ref, arrived)
    copy.start()
    weight_rows = weight_ref.shape[0]
    head_width = HEADS * HD
    room[...] = jnp.zeros_like(room)
    for y in range(4):
        first = y * YW
        split = HALF - YW
        for core in range(2):
            slot = y * 2 + core
            base = (core + 1) * head_width
            size = min(YW, head_width - first)
            room[slot, :weight_rows, :size] = weight_ref[:, base + first : base + first + size].astype(F32)
            begin = first + core * split
            query_size = min(YW - split if core else split, head_width - begin)
            room[slot, :weight_rows, YW : YW + query_size] = weight_ref[
                :, begin : begin + query_size
            ].astype(F32)
            text = text_ref[core, :, first : first + size].astype(F32)
            room[slot, 19:24, :size] = text[:5]
            room[slot, 19:22, YW:] = text[5:8, :split]
            if size > split:
                room[slot, 22:23, YW : YW + size - split] = text[5:6, split:size]
                room[slot, 23:24, YW : YW + size - split] = text[6:7, split:size]
                room[slot, 22:23, YW + 128 :] = text[7:8, split : split + 64]
            if size == YW:
                room[slot, 23:24, YW + 128 :] = text[7:8, split + 64 :]
    out_ref[...] = room[...].astype(BF16)
    copy.wait()


def compact_kernel(received_ref, *refs):
    block_ref, text_ref, rows_room, text_room = refs[-4:]
    split = HALF - YW
    for source in range(8):
        value = received_ref[source].astype(F32)
        rows_room[source * 19 : (source + 1) * 19, :] = value[:19]
        at = source * TEXT_ROWS
        text_room[at : at + 5, :] = value[19:24, :YW]
        text_room[at + 5 : at + 8, :split] = value[19:22, YW:]
        text_room[at + 5 : at + 6, split:] = value[22:23, YW : YW + 128]
        text_room[at + 6 : at + 7, split:] = value[23:24, YW : YW + 128]
        text_room[at + 7 : at + 8, split : split + 64] = value[22:23, YW + 128 :]
        text_room[at + 7 : at + 8, split + 64 :] = value[23:24, YW + 128 :]
    block_ref[...] = rows_room[...].astype(BF16)
    text_ref[...] = text_room[...].astype(BF16)


def modulate_kernel(modulation, raw_ref, h_ref):
    wide = raw_ref[...].astype(F32)
    centred = wide - jnp.mean(wide, axis=-1, keepdims=True)
    normed = centred * lax.rsqrt(jnp.mean(centred * centred, axis=-1, keepdims=True) + EPSILON)
    modulated = normed * (1.0 + modulation[1]) + modulation[0]
    modulated = modulated.astype(BF16)
    h_ref[...] = jnp.zeros_like(h_ref)
    for slot in range(16):
        h_ref[:, slot * SLOT : slot * SLOT + CHUNK] = modulated[:, slot * CHUNK : (slot + 1) * CHUNK]


def places_of_blocks():
    x = lax.axis_index("x")
    z = lax.axis_index("z1") * 2 + lax.axis_index("z0")
    slots = [x * 8 + z, (1 - x) * 8 + z]
    for step in range(1, 5):
        slots += [x * 8 + lax.rem(z + 8 - step, 8), (1 - x) * 8 + lax.rem(z + step, 8)]
        if step < 4:
            slots += [x * 8 + lax.rem(z + step, 8), (1 - x) * 8 + lax.rem(z + 8 - step, 8)]
    return slots


def project_kernel(gains_ref, h_ref, text_ref, *refs):
    blocks, (pairs_ref, queries_ref, whole, gain_ref) = refs[:16], refs[16:]
    y, core = lax.axis_index("y"), lax.axis_index("core")
    split = HALF - YW
    gain_ref[...] = jnp.ones_like(gain_ref)
    for at in range(4):
        first = at * YW
        size = min(YW, HEADS * HD - first)

        @pl.when((y == at) & (core == 0))
        def _():
            gain_ref[:, :size] = gains_ref[1:2, first : first + size]
            gain_ref[:, YW:] = gains_ref[0:1, first : first + split]

        @pl.when((y == at) & (core == 1))
        def _():
            gain_ref[:, YW : YW + size - split] = gains_ref[0:1, first + split : first + size]

    whole[:, CHUNK:, :] = jnp.zeros((16, SLOT - CHUNK, HALF), BF16)
    for slot, block in zip(places_of_blocks(), blocks):
        whole[slot, :CHUNK, :] = block[...]
    rows = h_ref.shape[0]
    shard = pairs_ref.shape[0] * 2 // YH
    half = shard // 2
    pairs_ref[rows:shard, :] = text_ref[:, :128]
    pairs_ref[shard + rows : 2 * shard, :] = text_ref[:, 128:256]
    pairs_ref[shard + half + rows :, HD:] = text_ref[:, 256:]
    low = lax.broadcasted_iota(jnp.int32, (rows, 128), 1) < HD
    for tile in range(0, HALF, 256):
        weights = whole[:, :, tile : tile + 256].reshape(16 * SLOT, 256)
        product = jnp.dot(h_ref[...], weights, preferred_element_type=F32)
        for part in range(2):
            begin = tile + part * 128
            columns = slice(begin, begin + 128)
            value = product[:, part * 128 : part * 128 + 128]
            square = value * value
            low_sum = jnp.sum(jnp.where(low, square, 0.0), axis=-1, keepdims=True)
            high_sum = jnp.sum(jnp.where(low, 0.0, square), axis=-1, keepdims=True)
            mean = jnp.where(low, low_sum, high_sum) * (1.0 / HD)
            scaled = value * lax.rsqrt(mean + EPSILON) * gain_ref[:, columns]
            column = lax.broadcasted_iota(jnp.int32, (1, 128), 1) + begin
            plain = (core == 1) & (column < YW)
            result = jnp.where(plain, value, scaled).astype(BF16)
            if begin + 128 <= YW:
                pairs_ref[begin // 128 * shard : begin // 128 * shard + rows, :] = result
            elif begin < YW:
                pairs_ref[2 * shard :, :HD] = result[:half, :HD]
                pairs_ref[2 * shard : shard + half + rows, HD:] = result[half:, :HD]
                queries_ref[:, :HD] = result[:, HD:]
            else:
                queries_ref[:, begin - YW : begin + 128 - YW] = result


def unpack(packed, room, part):
    shard = packed.shape[0] * 2 // YH
    half = shard // 2
    begin = part * shard
    room[0, begin : begin + shard, :] = packed[:shard, :]
    room[1, begin : begin + shard, :] = packed[shard : 2 * shard, :]
    room[2, begin : begin + half, :HD] = packed[2 * shard :, :HD]
    room[2, begin + half : begin + shard, :HD] = packed[2 * shard :, HD:]


def attend_kernel(counts_ref, own, beside, own_q, beside_q, far, far_beside, out_ref, keys, values):
    core, z0 = lax.axis_index("core"), lax.axis_index("z0")
    text_valid = counts_ref[lax.axis_index("x") * 4 + lax.axis_index("z1")]
    shard = own.shape[0] * 2 // YH
    rows = out_ref.shape[0] * 2 // YH
    image = shard - 8 * TEXT_ROWS
    for part, (mine, other) in enumerate(((own, beside), (far, far_beside))):

        @pl.when(core == 0)
        def _():
            unpack(mine, keys, part)
            unpack(other, values, part)

        @pl.when(core == 1)
        def _():
            unpack(other, keys, part)
            unpack(mine, values, part)

    column = lax.broadcasted_iota(jnp.int32, (1, 2 * shard), 1)
    is_far = column >= shard
    column = jnp.where(is_far, column - shard, column)
    slot = column - image + 8 * TEXT_ROWS * jnp.where(is_far, 1 - z0, z0)
    bias = jnp.where((column < image) | (slot < text_valid), 0.0, MASKED).astype(F32)
    split = HALF - YW
    each = rows // 4
    half = rows // 2
    places = [pl.ds(pl.multiple_of((2 * y + core) * each, 16), each) for y in range(4)]
    mine, other = (
        jnp.concatenate([ref[at, :] for at in places], 0) for ref in (own_q, beside_q)
    )
    first = jnp.where(core == 0, mine, other)
    second = jnp.where(core == 0, other, mine)
    for head in range(YH):
        columns = slice(head * HD, (head + 1) * HD)
        lanes = head % 2 * HD
        if head * HD < split:
            queries = first[:, columns]
        else:
            queries = second[:, head * HD - split : (head + 1) * HD - split]
        scores = lax.dot_general(
            queries * BF16(HD**-0.5),
            keys[head // 2, :, lanes : lanes + HD],
            (((1,), (1,)), ((), ())),
            preferred_element_type=F32,
        )
        scores = scores + bias
        peak = jnp.max(scores, axis=-1, keepdims=True)
        weights = jnp.exp(scores - peak)
        totals = jnp.sum(weights, axis=-1, keepdims=True)
        mixed = jnp.dot(
            weights.astype(BF16),
            values[head // 2, :, lanes : lanes + HD],
            preferred_element_type=F32,
        )
        attended = (mixed / totals).astype(BF16)
        at = head // 2 * rows
        if head < YH - 1:
            out_ref[at : at + rows, lanes : lanes + HD] = attended
        else:
            out_ref[at : at + half, :HD] = attended[:half]
            out_ref[at : at + half, HD:] = attended[half:]


def arrange_kernel(gathered_ref, out_ref, weights):
    each = weights.shape[0] // 32
    gap = gathered_ref.shape[0] // 16
    for place in range(16):
        value = gathered_ref[place * gap : (place + 1) * gap, :].astype(F32)
        core, z = divmod(place, 8)
        for x in range(2):
            at = ((x * 8 + z) * 2 + core) * each
            weights[at : at + each, :] = value[x * each : (x + 1) * each]
    out_ref[...] = weights[...].astype(BF16)


def finish_kernel(a0, a1, a2, a3, weight_ref, o0, o1, o2, o3, heads, result):
    y = lax.axis_index("y")
    rows = a0.shape[0] * 2 // YH
    half = rows // 2
    for by, attended in enumerate((a0, a1, a2, a3)):
        place = lax.rem(y + 4 - by, 4)
        heads[place, :, :128] = attended[:rows, :]
        heads[place, :, 128:256] = attended[rows : 2 * rows, :]
        heads[place, :half, 256:YW] = attended[2 * rows :, :HD]
        heads[place, half:, 256:YW] = attended[2 * rows :, HD:]
    total = None
    for q in range(4):
        size = min(YW, HEADS * HD - q * YW)
        part = lax.dot_general(
            heads[q][:, :size],
            weight_ref[:, q * YW : q * YW + size],
            (((1,), (1,)), ((), ())),
            preferred_element_type=F32,
        )
        total = part if total is None else total + part
    rows = o0.shape[0]
    result[...] = total.astype(BF16).reshape(4, rows, total.shape[1])
    for by, out_ref in enumerate((o0, o1, o2, o3)):
        out_ref[...] = result[lax.rem(y + by, 4)]


def place_columns(part, by, branch):
    y = lax.axis_index("y")
    run = part.shape[1] // 16
    value = part[...].astype(F32)
    for q in range(4):

        @pl.when(lax.rem(y + 4 - by, 4) == q)
        def _():
            for m in range(16):
                at = (m * 4 + q) * run
                branch[:, at : at + run] = value[:, m * run : (m + 1) * run]


def assemble_early_kernel(n0, n1, n3, branch):
    for by, part in ((0, n0), (1, n1), (3, n3)):
        place_columns(part, by, branch)


def assemble_kernel(modulation, raw_ref, early_ref, n2, out_ref, branch):
    branch[...] = early_ref[...]
    place_columns(n2, 2, branch)
    out_ref[...] = (raw_ref[...].astype(F32) + modulation[2] * branch[...]).astype(BF16)


def in_vmem(kernel, out_shape, args, flops=0, scratch=(), scalars=0, after=(), anywhere=(), limit=8):
    size = sum(a.size * a.dtype.itemsize for a in args)
    vmem = pl.BlockSpec(memory_space=pltpu.VMEM)
    return pl.pallas_call(
        kernel,
        out_shape=out_shape,
        in_specs=[pl.BlockSpec(memory_space=pltpu.SMEM)] * scalars
        + [vmem] * (len(args) - scalars)
        + [pl.BlockSpec(memory_space=pl.ANY)] * len(anywhere)
        + [vmem] * len(after),
        out_specs=jax.tree.map(lambda _: vmem, out_shape),
        scratch_shapes=list(scratch),
        compiler_params=pltpu.CompilerParams(vmem_limit_bytes=limit * 1024 * 1024),
        cost_estimate=pl.CostEstimate(flops=flops, bytes_accessed=size, transcendentals=0),
    )(*args, *anywhere, *after)


def per_device(
    stale_states, mod_table, timesteps, text_count, text_kv, qkv_weight, out_weight, qk_gain
):
    rows, width = stale_states.shape[1:]
    head_width = HEADS * HD
    weight_rows = qkv_weight.shape[1]
    quarter = width // 4
    split = HALF - YW

    halves, modulation = in_vmem(
        prepare_kernel,
        (jax.ShapeDtypeStruct((8, 24, HALF), BF16), jax.ShapeDtypeStruct((3, 1, width), F32)),
        (timesteps, qkv_weight[0], text_kv),
        scratch=[pltpu.VMEM((8, 24, HALF), F32), pltpu.SemaphoreType.DMA],
        scalars=1,
        anywhere=(mod_table.reshape(mod_table.shape[1:3] + (1, width)),),
        limit=60,
    )
    received = lax.all_to_all(halves, ("y", "core"), split_axis=0, concat_axis=0, tiled=True)
    shard = jnp.transpose(out_weight[0])

    raw = permuted(stale_states[0], "comp", 1)
    h = in_vmem(
        modulate_kernel, jax.ShapeDtypeStruct((rows, 16 * SLOT), BF16), (modulation, raw)
    )
    block, text = in_vmem(
        compact_kernel,
        (
            jax.ShapeDtypeStruct((CHUNK, HALF), BF16),
            jax.ShapeDtypeStruct((8 * TEXT_ROWS, YW), BF16),
        ),
        (received,),
        flops=7 * 10**10,
        scratch=[pltpu.VMEM((CHUNK, HALF), F32), pltpu.VMEM((8 * TEXT_ROWS, YW), F32)],
        after=(h,),
    )
    h = lax.all_gather(h, ("y", "core"), axis=0, tiled=True)

    ahead = lambda part: permuted(part, Z, 1)
    behind = lambda part: permuted(part, Z, 7)
    other = permuted(block, "x", 1)
    own_aheads, own_behinds = [ahead(block)], [behind(block)]
    other_aheads, other_behinds = [ahead(other)], [behind(other)]
    for step in range(2, 5):
        own_aheads.append(ahead(own_aheads[-1]))
        other_behinds.append(behind(other_behinds[-1]))
        if step < 4:
            own_behinds.append(behind(own_behinds[-1]))
            other_aheads.append(ahead(other_aheads[-1]))
    blocks = [block, other]
    for step in range(1, 5):
        blocks += [own_aheads[step - 1], other_behinds[step - 1]]
        if step < 4:
            blocks += [own_behinds[step - 1], other_aheads[step - 1]]

    shard_beside = permuted(hold(shard, block), "x", 1)
    both = in_vmem(
        beside_kernel,
        jax.ShapeDtypeStruct((40, head_width), BF16),
        (shard, shard_beside),
        scratch=[pltpu.VMEM((40, head_width), F32)],
        after=(own_aheads[1], own_behinds[1], other_aheads[0], other_behinds[0]),
    )
    out_columns = lax.all_gather(both, ("core", "z1", "z0"), axis=0, tiled=True)

    shard_rows = 8 * (rows + TEXT_ROWS)
    pairs, queries = in_vmem(
        project_kernel,
        (
            jax.ShapeDtypeStruct((shard_rows // 2 * YH, 128), BF16),
            jax.ShapeDtypeStruct((8 * rows, split), BF16),
        ),
        (qk_gain[0], h, text, *blocks),
        flops=2 * 8 * rows * 16 * SLOT * HALF,
        scratch=[
            pltpu.VMEM((16, SLOT, HALF), BF16),
            pltpu.VMEM((1, HALF), F32),
        ],
    )

    far = permuted(pairs, "z0", 1)
    attended = in_vmem(
        attend_kernel,
        jax.ShapeDtypeStruct((2 * rows * YH, 128), BF16),
        (
            text_count,
            pairs,
            permuted(pairs, "core", 1),
            queries,
            permuted(queries, "core", 1),
            far,
            permuted(far, "core", 1),
        ),
        flops=4 * 4 * rows * 2 * shard_rows * YW,
        scratch=[pltpu.VMEM((3, 2 * shard_rows, 128), BF16)] * 2,
        scalars=1,
    )

    out_columns = in_vmem(
        arrange_kernel,
        jax.ShapeDtypeStruct((32 * weight_rows, head_width), BF16),
        (out_columns,),
        flops=10**10,
        scratch=[pltpu.VMEM((32 * weight_rows, head_width), F32)],
    )
    gathered = tuple(permuted(attended, "y", by) for by in (1, 2, 3))
    parts = in_vmem(
        finish_kernel,
        (jax.ShapeDtypeStruct((rows, quarter), BF16),) * 4,
        (attended,)
        + gathered
        + (out_columns,),
        flops=2 * 4 * rows * head_width * quarter,
        scratch=[
            pltpu.VMEM((4, 4 * rows, YW), BF16),
            pltpu.VMEM((4, rows, quarter), BF16),
        ],
    )
    parts = [parts[0]] + [permuted(parts[by], "y", by) for by in (1, 2, 3)]
    early = in_vmem(
        assemble_early_kernel,
        jax.ShapeDtypeStruct((rows, width), F32),
        (parts[0], parts[1], parts[3]),
        flops=10**10,
    )
    new = in_vmem(
        assemble_kernel,
        jax.ShapeDtypeStruct((rows, width), BF16),
        (modulation, raw, early, parts[2]),
        scratch=[pltpu.VMEM((rows, width), F32)],
    )
    return new[None]


def solution(mesh):
    fine = Mesh(np.asarray(mesh.devices).reshape(SIZES), AXES)
    in_specs = (
        P("comp", SEQ, None),
        P("comp", None, None, None),
        P(),
        P(),
        P(None, SEQ, None),
        P("comp", SEQ, None),
        P("comp", None, SEQ),
        P("comp", None, None),
    )
    return jax.shard_map(
        per_device, mesh=fine, in_specs=in_specs, out_specs=P("comp", SEQ, None), check_vma=False
    )
```
